32 devices in a mesh: parts: 2 (over y), tm: 4 (over z), dp: 4 (over x, core).
Axes of the slice: x: 2, y: 2, z: 4, core: 2. Of those that a mesh axis runs over, the one named last changes fastest.
Arguments:
- signal: bfloat16 [16, 512, 2048], P(('parts', 'dp'), 'tm'), parts along dimension 0, may hold values from -112 to 112
- weight: float32 [640, 2048], P('parts', 'tm'), parts along dimension 0, may hold values from -0.3125 to 0.3125
- first_moment: float32 [640, 2048], P('parts', 'tm'), parts along dimension 0, may hold values from -0.625 to 0.625
- second_moment: float32 [640, 2048], P('parts', 'tm'), parts along dimension 0, may hold values from 0.001 to 0.01
- shuffle: int32 [2048], replicated, may hold values from 0 to 2047, each once
Outputs:
- reconstruction: bfloat16 [16, 512, 2048], P(('parts', 'dp'), 'tm'), parts along dimension 0
- mean_error: float32 [2], P('parts'), parts along dimension 0
- direction: float32 [640, 2048], P('parts', 'tm'), parts along dimension 0
- back_pre: bfloat16 [16, 512, 2048], P(('parts', 'dp'), 'tm'), parts along dimension 0
The draws below stay inside these ranges and needn't reach their ends.
There are 2 independent parts, one for each index of `parts`. The reference program is written for one: setup_inputs(seed, part) draws one part's arguments, and reference() takes and returns one part's arrays. A program takes and returns all parts, laid end to end along the dimension named above; an argument that names none is the same for every part. Nothing has to cross between parts.
All inputs are finite; a program needn't handle non-finite values.
Results may differ from the reference program's by a relative error of at most 0.0066.
Values may be sent and summed in bfloat16 or wider, within the bound.
A program may use at most 64 MiB of HBM per device.

```python
import math
import jax
import jax.numpy as jnp
from jax import lax

GW = 64
GROUPS = 32
KERNEL = 5
CH = 2048
KW = 320
LEN = 512
BATCH = 8


def draw_signal(key, part):
    key_noise, key_rows, key_cols = jax.random.split(key, 3)
    times = jnp.arange(LEN, dtype=jnp.float32) / LEN
    channels = jnp.arange(CH, dtype=jnp.int32)
    col_base = 0.5 * (channels // GW).astype(jnp.float32) / GROUPS + 0.5 * (channels % GW).astype(jnp.float32) / GW
    seq_pos = jnp.arange(BATCH, dtype=jnp.float32) / BATCH
    row_rough = jax.random.uniform(key_rows, (BATCH, LEN, 1), jnp.float32, 0.8, 1.25)
    col_rough = jax.random.uniform(key_cols, (CH,), jnp.float32, 0.8, 1.25)
    row_scale = 10.0 ** (times - 0.5)
    col_scale = 10.0 ** (col_base - 0.5) * col_rough
    noise = jax.random.truncated_normal(key_noise, -4.0, 4.0, (BATCH, LEN, CH), jnp.float32)
    seq_scale = 3.0 ** (seq_pos - 0.5)
    values = noise * row_rough * row_scale[None, :, None] * col_scale[None, None, :] * seq_scale[:, None, None]
    return values.astype(jnp.bfloat16)


def steps_of(stream_key, extent, cuts, low, top_value):
    def one(dim, blocks):
        heights = jax.random.uniform(jax.random.fold_in(jax.random.fold_in(stream_key, 6), dim), (blocks,), jnp.float32, low / len(cuts), top_value / len(cuts))
        return jnp.repeat(jnp.exp(heights), extent[dim] // blocks).reshape((-1,) + (1,) * (len(extent) - dim - 1))

    factor_of = one(*cuts[0])
    for cut in cuts[1:]:
        factor_of = factor_of * one(*cut)
    return factor_of


def normal_values(rng, shape, spread, bound, shards=(), kind=jnp.bfloat16):
    drawn = spread * jax.random.normal(rng, shape, jnp.float32)
    if shards:
        drawn = drawn * steps_of(rng, shape, shards, -0.22, 0.18)
    return jnp.clip(drawn, -bound, bound).astype(kind)


def setup_inputs(seed: int = 0, part: int = 0) -> dict:
    keys = jax.random.split(jax.random.key(seed), 6)
    part_splits = jax.random.split(jax.random.fold_in(keys[5], part), 6)
    signal = draw_signal(jax.random.fold_in(jax.random.fold_in(keys[5], part), 71), part)
    weight = normal_values(part_splits[1], (KW, CH), KW ** -0.5, 0.3125, ((1, 4),), jnp.float32)
    first_moment = normal_values(part_splits[2], (KW, CH), 0.1, 0.625, ((1, 4),), jnp.float32)
    second_moment = jnp.clip(jnp.exp(math.log(0.01) - 2.30258502 * jax.random.uniform(part_splits[3], (KW, CH), jnp.float32) ** steps_of(part_splits[3], (KW, CH), ((1, 4),), -0.2, 0.2)), 0.001, 0.01)
    shuffle = jax.random.permutation(keys[4], CH).astype(jnp.int32)
    return dict(signal=signal, weight=weight, first_moment=first_moment, second_moment=second_moment, shuffle=shuffle)


beta_one = 0.9
beta_two = 0.999
adam_eps = 1e-08
decay_rate = 0.1
rms_eps = 1e-06
step_count = 100

def taps_forward(padded, taps_grid, length):
    batch_rows = padded.shape[0]
    kernel = taps_grid.shape[0]
    group_size = taps_grid.shape[1]
    groups = taps_grid.shape[2]
    summed = jnp.zeros((batch_rows, length, groups, group_size), jnp.float32)
    for offset in range(kernel):
        window = padded[:, offset:offset + length].reshape(batch_rows, length, groups, group_size)
        summed = summed + jnp.einsum('stgi,igo->stgo', window.astype(jnp.float32), taps_grid[offset].astype(jnp.float32))
    return summed.reshape(batch_rows, length, groups * group_size)

def taps_backward(padded, taps_grid, length):
    batch_rows = padded.shape[0]
    kernel = taps_grid.shape[0]
    group_size = taps_grid.shape[1]
    groups = taps_grid.shape[2]
    summed = jnp.zeros((batch_rows, length, groups, group_size), jnp.float32)
    for offset in range(kernel):
        start = kernel - 1 - offset
        window = padded[:, start:start + length].reshape(batch_rows, length, groups, group_size)
        summed = summed + jnp.einsum('stgo,igo->stgi', window.astype(jnp.float32), taps_grid[offset].astype(jnp.float32))
    return summed.reshape(batch_rows, length, groups * group_size)

def taps_gradient(padded_signal, padded_mixed, back_pre, error_bf, taps_grid, length):
    batch_rows = padded_signal.shape[0]
    kernel = taps_grid.shape[0]
    group_size = taps_grid.shape[1]
    groups = taps_grid.shape[2]
    back_grid = back_pre.reshape(batch_rows, length, groups, group_size).astype(jnp.float32)
    error_grid = error_bf.reshape(batch_rows, length, groups, group_size).astype(jnp.float32)
    columns = []
    for offset in range(kernel):
        start = kernel - 1 - offset
        inputs = padded_signal[:, offset:offset + length].reshape(batch_rows, length, groups, group_size)
        mixed = padded_mixed[:, start:start + length].reshape(batch_rows, length, groups, group_size)
        encoder_part = jnp.einsum('stgi,stgo->igo', inputs.astype(jnp.float32), back_grid)
        decoder_part = jnp.einsum('stgo,stgi->igo', mixed.astype(jnp.float32), error_grid)
        columns.append(encoder_part + decoder_part)
    return jnp.stack(columns).reshape(kernel * group_size, groups * group_size)

def silu_slope(pre):
    sigma = jax.nn.sigmoid(pre)
    return sigma * (1.0 + pre * (1.0 - sigma))

def adam_direction(grad_part, square_total, entries, weight_part, first_part, second_part):
    rms_value = jnp.sqrt(square_total / entries + rms_eps)
    factor = jnp.minimum(1.0, 1.0 / rms_value)
    clipped = grad_part * factor
    first_new = beta_one * first_part + (1.0 - beta_one) * clipped
    second_new = beta_two * second_part + (1.0 - beta_two) * clipped * clipped
    first_hat = first_new / (1.0 - beta_one ** step_count)
    second_hat = second_new / (1.0 - beta_two ** step_count)
    return first_hat / (jnp.sqrt(second_hat) + adam_eps) + decay_rate * weight_part

def reference(signal, weight, first_moment, second_moment, shuffle):
    margin = (KERNEL - 1) // 2
    taps_grid = weight.astype(jnp.bfloat16).reshape(KERNEL, GW, GROUPS, GW)
    inverse = jnp.zeros((CH,), jnp.int32).at[shuffle].set(jnp.arange(CH, dtype=jnp.int32))
    edges = ((0, 0), (margin, margin), (0, 0))

    def one_window(carry, window_signal):
        grad_sum, square_sum = carry
        signal_one = window_signal[None]
        padded_signal = jnp.pad(signal_one, edges)
        pre = taps_forward(padded_signal, taps_grid, LEN)
        activation = jax.nn.silu(pre).astype(jnp.bfloat16)
        mixed = jnp.take(activation, shuffle, axis=2)
        padded_mixed = jnp.pad(mixed, edges)
        decoded = taps_backward(padded_mixed, taps_grid, LEN)
        error = decoded - signal_one.astype(jnp.float32)
        error_bf = error.astype(jnp.bfloat16)
        padded_error = jnp.pad(error_bf, edges)
        back_mixed = taps_forward(padded_error, taps_grid, LEN)
        back_pre = (jnp.take(back_mixed, inverse, axis=2) * silu_slope(pre)).astype(jnp.bfloat16)
        gradient = taps_gradient(padded_signal, padded_mixed, back_pre, error_bf, taps_grid, LEN)
        return ((grad_sum + gradient, square_sum + jnp.sum(error * error)), (decoded.astype(jnp.bfloat16)[0], back_pre[0]))
    start_carry = (jnp.zeros((KW, CH), jnp.float32), jnp.zeros((), jnp.float32))
    (gradient, square_sum), (reconstruction, back_pre) = lax.scan(one_window, start_carry, signal)
    mean_error = (square_sum / (BATCH * LEN * CH)).reshape(1)
    square_total = jnp.sum(gradient * gradient)
    direction = adam_direction(gradient, square_total, KW * CH, weight, first_moment, second_moment)
    return (reconstruction, mean_error, direction, back_pre)
```

```python
import functools

import jax
import jax.numpy as jnp
from jax import lax
from jax.experimental import pallas as pl
from jax.experimental.pallas import tpu as pltpu
from jax.sharding import PartitionSpec as P

GW = 64
KERNEL = 5
CH = 2048
KW = 320
WIDE = 256
HALO = 8

beta_one = 0.9
beta_two = 0.999
adam_eps = 1e-08
decay_rate = 0.1
rms_eps = 1e-06
step_count = 100

TN = (((0,), (0,)), ((), ()))
NT = (((1,), (1,)), ((), ()))


def shifted(value, amount):
    rows = value.shape[0]
    return value if amount % rows == 0 else pltpu.roll(value, amount % rows, 0)


def local_part(value, windows, length):
    step = length + 2 * HALO
    return jnp.concatenate(
        [value[w * step + HALO : w * step + HALO + length] for w in range(windows)], axis=0
    )


def spread_part(value, windows, length):
    blank = jnp.zeros((HALO, value.shape[1]), value.dtype)
    pieces = []
    for w in range(windows):
        pieces += [blank, value[w * length : (w + 1) * length], blank]
    return jnp.concatenate(pieces, axis=0)


def diagonal(value):
    lane = lax.broadcasted_iota(jnp.int32, (GW, WIDE), 1) // GW
    picked = value[:GW]
    for j in range(1, WIDE // GW):
        picked = jnp.where(lane == j, value[j * GW : (j + 1) * GW], picked)
    return picked


def compute_kernel(
    windows, length, sig_ref, w_ref, shuffle_ref, rec_ref, back_ref, grad_ref, square_ref,
    onehot, table, pre, act, back, partial,
):
    channels = sig_ref.shape[1]
    blocks = channels // WIDE
    rows = sig_ref.shape[0]
    step = length + 2 * HALO
    me, peers = lax.axis_index("tm"), lax.axis_size("tm")
    place = lax.broadcasted_iota(jnp.int32, (rows, WIDE), 0)
    inner = lax.rem(place, step)
    low = jnp.where(me == 0, HALO, 0)
    high = jnp.where(me == peers - 1, HALO + length, step)
    inside = jnp.logical_and(inner >= low, inner < high)
    block_mask = (
        lax.broadcasted_iota(jnp.int32, (WIDE, WIDE), 0) // GW
        == lax.broadcasted_iota(jnp.int32, (WIDE, WIDE), 1) // GW
    )
    square_ref[...] = jnp.zeros_like(square_ref)

    def encode(index, carry):
        cols = pl.ds(pl.multiple_of(index * WIDE, WIDE), WIDE)
        for k in range(KERNEL):
            taps = w_ref[k * GW : (k + 1) * GW, cols].astype(jnp.float32)
            tiled = jnp.concatenate([taps] * (WIDE // GW), axis=0)
            table[index, k * WIDE : (k + 1) * WIDE, :] = jnp.where(block_mask, tiled, 0.0).astype(
                jnp.bfloat16
            )
        x = sig_ref[:, cols].astype(jnp.float32)
        stack = jnp.concatenate(
            [shifted(x, 2 - k).astype(jnp.bfloat16) for k in range(KERNEL)], axis=1
        )
        value = jnp.dot(stack, table[index], preferred_element_type=jnp.float32)
        pre[:, cols] = local_part(value, windows, length)
        active = value / (1.0 + jnp.exp(-value))
        act[:, cols] = jnp.where(inside, active, 0.0).astype(jnp.bfloat16)
        return carry

    lax.fori_loop(0, blocks, encode, 0)

    def decode(index, carry):
        cols = pl.ds(pl.multiple_of(index * WIDE, WIDE), WIDE)
        source = lax.broadcasted_iota(jnp.int32, (channels, WIDE), 0)
        onehot[:, cols] = jnp.where(source == shuffle_ref[:, cols], 1.0, 0.0).astype(jnp.bfloat16)
        mixed = jnp.dot(act[...], onehot[:, cols], preferred_element_type=jnp.float32)
        decoded = jnp.zeros((rows, WIDE), jnp.float32)
        own_mixed = []
        for k in range(KERNEL):
            moved = shifted(mixed, k - 2)
            own_mixed.append(local_part(moved, windows, length).astype(jnp.bfloat16))
            decoded += lax.dot_general(
                moved.astype(jnp.bfloat16),
                table[index, k * WIDE : (k + 1) * WIDE, :],
                NT,
                preferred_element_type=jnp.float32,
            )
        error = jnp.where(inside, decoded - sig_ref[:, cols].astype(jnp.float32), 0.0)
        own_decoded = local_part(decoded, windows, length).astype(jnp.bfloat16)
        for w in range(windows):
            rec_ref[w, :, cols] = own_decoded[w * length : (w + 1) * length]
        own_error = local_part(error, windows, length)
        square_ref[...] += (own_error * own_error).reshape(-1, 8, WIDE).sum(axis=0)
        stack = jnp.concatenate(
            [shifted(error, 2 - k).astype(jnp.bfloat16) for k in range(KERNEL)], axis=1
        )
        value = jnp.dot(stack, table[index], preferred_element_type=jnp.float32)
        back[:, cols] = local_part(value, windows, length).astype(jnp.bfloat16)
        product = lax.dot_general(
            own_error.astype(jnp.bfloat16),
            jnp.concatenate(own_mixed, axis=1),
            TN,
            preferred_element_type=jnp.float32,
        )
        for k in range(KERNEL):
            partial[k * GW : (k + 1) * GW, cols] = diagonal(product[:, k * WIDE : (k + 1) * WIDE])
        return carry

    lax.fori_loop(0, blocks, decode, 0)

    def finish(index, carry):
        start = pl.multiple_of(index * WIDE, WIDE)
        cols = pl.ds(start, WIDE)
        restored = lax.dot_general(
            back[...], onehot[pl.ds(start, WIDE), :], NT, preferred_element_type=jnp.float32
        )
        value = pre[:, cols]
        sigma = 1.0 / (1.0 + jnp.exp(-value))
        own = (restored * (sigma * (1.0 + value * (1.0 - sigma)))).astype(jnp.bfloat16)
        for w in range(windows):
            back_ref[w, :, cols] = own[w * length : (w + 1) * length]
        wide = spread_part(own.astype(jnp.float32), windows, length)
        stack = jnp.concatenate(
            [shifted(wide, k - 2).astype(jnp.bfloat16) for k in range(KERNEL)], axis=1
        )
        product = lax.dot_general(
            sig_ref[:, cols], stack, TN, preferred_element_type=jnp.float32
        )
        for k in range(KERNEL):
            taken = slice(k * GW, (k + 1) * GW)
            total = partial[taken, cols] + diagonal(product[:, k * WIDE : (k + 1) * WIDE])
            grad_ref[taken, cols] = total.astype(grad_ref.dtype)
        return carry

    lax.fori_loop(0, blocks, finish, 0)


def local_step(signal, weight, shuffle, before, after):
    windows, length, channels = signal.shape
    wide = jnp.concatenate([before, signal, after], axis=1)
    rows = windows * (length + 2 * HALO)
    vmem = pl.BlockSpec(memory_space=pltpu.VMEM)
    own = windows * length
    return pl.pallas_call(
        functools.partial(compute_kernel, windows, length),
        out_shape=(
            jax.ShapeDtypeStruct(signal.shape, jnp.bfloat16),
            jax.ShapeDtypeStruct(signal.shape, jnp.bfloat16),
            jax.ShapeDtypeStruct((KERNEL * GW, channels), jnp.bfloat16),
            jax.ShapeDtypeStruct((8, WIDE), jnp.float32),
        ),
        in_specs=[vmem] * 3,
        out_specs=(vmem,) * 4,
        scratch_shapes=[
            pltpu.VMEM((channels, channels), jnp.bfloat16),
            pltpu.VMEM((channels // WIDE, KERNEL * WIDE, WIDE), jnp.bfloat16),
            pltpu.VMEM((own, channels), jnp.float32),
            pltpu.VMEM((rows, channels), jnp.bfloat16),
            pltpu.VMEM((own, channels), jnp.bfloat16),
            pltpu.VMEM((KERNEL * GW, channels), jnp.float32),
        ],
        compiler_params=pltpu.CompilerParams(vmem_limit_bytes=48 * 1024 * 1024),
    )(wide.reshape(rows, channels), weight, shuffle.reshape(1, channels))


def adam_direction(grad_part, square_total, entries, weight_part, first_part, second_part):
    rms_value = jnp.sqrt(square_total / entries + rms_eps)
    factor = jnp.minimum(1.0, 1.0 / rms_value)
    clipped = grad_part * factor
    first_new = beta_one * first_part + (1.0 - beta_one) * clipped
    second_new = beta_two * second_part + (1.0 - beta_two) * clipped * clipped
    first_hat = first_new / (1.0 - beta_one**step_count)
    second_hat = second_new / (1.0 - beta_two**step_count)
    return first_hat / (jnp.sqrt(second_hat) + adam_eps) + decay_rate * weight_part


def on_device(signal, weight, first_moment, second_moment, shuffle):
    windows, length, channels = signal.shape
    peers = lax.axis_size("tm")
    up = [(i, i + 1) for i in range(peers - 1)]
    down = [(j, i) for i, j in up]
    before = lax.ppermute(signal[:, length - HALO :], "tm", up)
    after = lax.ppermute(signal[:, :HALO], "tm", down)
    full_weight = lax.all_gather(weight.astype(jnp.bfloat16), "tm", axis=1, tiled=True)
    decoded, back_pre, gradient, squares = local_step(signal, full_weight, shuffle, before, after)
    square_sum = lax.psum(jnp.sum(squares), ("tm", "dp"))
    element_count = windows * lax.axis_size("dp") * length * peers * channels
    mean_error = (square_sum / element_count).reshape(1)
    owned = lax.psum_scatter(gradient, "tm", scatter_dimension=1, tiled=True)
    owned = lax.psum(owned, "dp").astype(jnp.float32)
    square_total = lax.psum(jnp.sum(owned * owned), "tm")
    direction = adam_direction(owned, square_total, KW * CH, weight, first_moment, second_moment)
    return (decoded, mean_error, direction, back_pre)


def solution(mesh):
    return jax.shard_map(
        on_device,
        mesh=mesh,
        in_specs=(
            P(("parts", "dp"), "tm", None),
            P("parts", "tm"),
            P("parts", "tm"),
            P("parts", "tm"),
            P(),
        ),
        out_specs=(
            P(("parts", "dp"), "tm", None),
            P("parts"),
            P("parts", "tm"),
            P(("parts", "dp"), "tm", None),
        ),
        check_vma=False,
    )
```

```python
import functools

import jax
import jax.numpy as jnp
from jax import lax
from jax.experimental import pallas as pl
from jax.experimental.pallas import tpu as pltpu
from jax.sharding import PartitionSpec as P

GW = 64
KERNEL = 5
CH = 2048
KW = 320
WIDE = 256
HALO = 8

beta_one = 0.9
beta_two = 0.999
adam_eps = 1e-08
decay_rate = 0.1
rms_eps = 1e-06
step_count = 100

MESH = pl.DeviceIdType.MESH
TN = (((0,), (0,)), ((), ()))
NT = (((1,), (1,)), ((), ()))


def shifted(value, amount):
    rows = value.shape[0]
    return value if amount % rows == 0 else pltpu.roll(value, amount % rows, 0)


def local_part(value, windows, length):
    step = length + 2 * HALO
    return jnp.concatenate(
        [value[w * step + HALO : w * step + HALO + length] for w in range(windows)], axis=0
    )


def spread_part(value, windows, length):
    blank = jnp.zeros((HALO, value.shape[1]), value.dtype)
    pieces = []
    for w in range(windows):
        pieces += [blank, value[w * length : (w + 1) * length], blank]
    return jnp.concatenate(pieces, axis=0)


def diagonal(value):
    lane = lax.broadcasted_iota(jnp.int32, (GW, WIDE), 1) // GW
    picked = value[:GW]
    for j in range(1, WIDE // GW):
        picked = jnp.where(lane == j, value[j * GW : (j + 1) * GW], picked)
    return picked


def compute_kernel(
    windows, length, sig_ref, w_ref, shuffle_ref, rec_ref, back_ref, grad_ref, square_ref,
    onehot, table, pre, act, back, partial,
):
    channels = sig_ref.shape[1]
    blocks = channels // WIDE
    rows = sig_ref.shape[0]
    step = length + 2 * HALO
    me, peers = lax.axis_index("tm"), lax.axis_size("tm")
    place = lax.broadcasted_iota(jnp.int32, (rows, WIDE), 0)
    inner = lax.rem(place, step)
    low = jnp.where(me == 0, HALO, 0)
    high = jnp.where(me == peers - 1, HALO + length, step)
    inside = jnp.logical_and(inner >= low, inner < high)
    block_mask = (
        lax.broadcasted_iota(jnp.int32, (WIDE, WIDE), 0) // GW
        == lax.broadcasted_iota(jnp.int32, (WIDE, WIDE), 1) // GW
    )
    square_ref[...] = jnp.zeros_like(square_ref)

    def encode(index, carry):
        cols = pl.ds(pl.multiple_of(index * WIDE, WIDE), WIDE)
        for k in range(KERNEL):
            taps = w_ref[index, k * GW : (k + 1) * GW, :].astype(jnp.float32)
            tiled = jnp.concatenate([taps] * (WIDE // GW), axis=0)
            table[index, k * WIDE : (k + 1) * WIDE, :] = jnp.where(block_mask, tiled, 0.0).astype(
                jnp.bfloat16
            )
        x = sig_ref[:, cols].astype(jnp.float32)
        stack = jnp.concatenate(
            [shifted(x, 2 - k).astype(jnp.bfloat16) for k in range(KERNEL)], axis=1
        )
        value = jnp.dot(stack, table[index], preferred_element_type=jnp.float32)
        pre[:, cols] = local_part(value, windows, length)
        active = value / (1.0 + jnp.exp(-value))
        act[:, cols] = jnp.where(inside, active, 0.0).astype(jnp.bfloat16)
        return carry

    lax.fori_loop(0, blocks, encode, 0)

    def decode(index, carry):
        cols = pl.ds(pl.multiple_of(index * WIDE, WIDE), WIDE)
        source = lax.broadcasted_iota(jnp.int32, (channels, WIDE), 0)
        onehot[:, cols] = jnp.where(source == shuffle_ref[:, cols], 1.0, 0.0).astype(jnp.bfloat16)
        mixed = jnp.dot(act[...], onehot[:, cols], preferred_element_type=jnp.float32)
        decoded = jnp.zeros((rows, WIDE), jnp.float32)
        own_mixed = []
        for k in range(KERNEL):
            moved = shifted(mixed, k - 2)
            own_mixed.append(local_part(moved, windows, length).astype(jnp.bfloat16))
            decoded += lax.dot_general(
                moved.astype(jnp.bfloat16),
                table[index, k * WIDE : (k + 1) * WIDE, :],
                NT,
                preferred_element_type=jnp.float32,
            )
        error = jnp.where(inside, decoded - sig_ref[:, cols].astype(jnp.float32), 0.0)
        own_decoded = local_part(decoded, windows, length).astype(jnp.bfloat16)
        for w in range(windows):
            rec_ref[w, :, cols] = own_decoded[w * length : (w + 1) * length]
        own_error = local_part(error, windows, length)
        square_ref[...] += (own_error * own_error).reshape(-1, 8, WIDE).sum(axis=0)
        stack = jnp.concatenate(
            [shifted(error, 2 - k).astype(jnp.bfloat16) for k in range(KERNEL)], axis=1
        )
        value = jnp.dot(stack, table[index], preferred_element_type=jnp.float32)
        back[:, cols] = local_part(value, windows, length).astype(jnp.bfloat16)
        product = lax.dot_general(
            own_error.astype(jnp.bfloat16),
            jnp.concatenate(own_mixed, axis=1),
            TN,
            preferred_element_type=jnp.float32,
        )
        for k in range(KERNEL):
            partial[k * GW : (k + 1) * GW, cols] = diagonal(product[:, k * WIDE : (k + 1) * WIDE])
        return carry

    lax.fori_loop(0, blocks, decode, 0)

    def finish(index, carry):
        start = pl.multiple_of(index * WIDE, WIDE)
        cols = pl.ds(start, WIDE)
        restored = lax.dot_general(
            back[...], onehot[pl.ds(start, WIDE), :], NT, preferred_element_type=jnp.float32
        )
        value = pre[:, cols]
        sigma = 1.0 / (1.0 + jnp.exp(-value))
        own = (restored * (sigma * (1.0 + value * (1.0 - sigma)))).astype(jnp.bfloat16)
        for w in range(windows):
            back_ref[w, :, cols] = own[w * length : (w + 1) * length]
        wide = spread_part(own.astype(jnp.float32), windows, length)
        stack = jnp.concatenate(
            [shifted(wide, k - 2).astype(jnp.bfloat16) for k in range(KERNEL)], axis=1
        )
        product = lax.dot_general(
            sig_ref[:, cols], stack, TN, preferred_element_type=jnp.float32
        )
        for k in range(KERNEL):
            taken = slice(k * GW, (k + 1) * GW)
            total = partial[taken, cols] + diagonal(product[:, k * WIDE : (k + 1) * WIDE])
            grad_ref[index, taken, :] = total.astype(grad_ref.dtype)
        return carry

    lax.fori_loop(0, blocks, finish, 0)


def local_step(signal, weight, shuffle, before, after):
    windows, length, channels = signal.shape
    wide = jnp.concatenate([before, signal, after], axis=1)
    rows = windows * (length + 2 * HALO)
    vmem = pl.BlockSpec(memory_space=pltpu.VMEM)
    own = windows * length
    return pl.pallas_call(
        functools.partial(compute_kernel, windows, length),
        out_shape=(
            jax.ShapeDtypeStruct(signal.shape, jnp.bfloat16),
            jax.ShapeDtypeStruct(signal.shape, jnp.bfloat16),
            jax.ShapeDtypeStruct((channels // WIDE, KERNEL * GW, WIDE), jnp.bfloat16),
            jax.ShapeDtypeStruct((8, WIDE), jnp.float32),
        ),
        in_specs=[vmem] * 3,
        out_specs=(vmem,) * 4,
        scratch_shapes=[
            pltpu.VMEM((channels, channels), jnp.bfloat16),
            pltpu.VMEM((channels // WIDE, KERNEL * WIDE, WIDE), jnp.bfloat16),
            pltpu.VMEM((own, channels), jnp.float32),
            pltpu.VMEM((rows, channels), jnp.bfloat16),
            pltpu.VMEM((own, channels), jnp.bfloat16),
            pltpu.VMEM((KERNEL * GW, channels), jnp.float32),
        ],
        compiler_params=pltpu.CompilerParams(vmem_limit_bytes=48 * 1024 * 1024),
    )(wide.reshape(rows, channels), weight, shuffle.reshape(1, channels))


def flip(index, bit):
    return index + bit - 2 * bit * ((index // bit) % 2)


def bits_of(count):
    return [1 << b for b in range(count.bit_length() - 1)]


def greet(peers, size, members, bits, mine):
    barrier = pltpu.get_barrier_semaphore()
    for j in range(1, size):
        pl.semaphore_signal(
            barrier, inc=1, device_id={"tm": lax.rem(peers + j, size)}, device_id_type=MESH
        )
    for bit in bits:
        pl.semaphore_signal(
            barrier, inc=1, device_id={"dp": flip(mine, bit)}, device_id_type=MESH
        )
    pl.semaphore_wait(barrier, size - 1 + len(bits))


def remote(src, dst, send, recv, target):
    return pltpu.make_async_remote_copy(
        src_ref=src, dst_ref=dst, send_sem=send, recv_sem=recv, device_id=target,
        device_id_type=MESH,
    )


def gather_kernel(
    size, members, shard_ref, first_ref, last_ref, full_ref, before_ref, after_ref,
    send_tm, recv_tm, send_dp, recv_dp, send_halo, recv_halo, local_sem,
):
    me, mine = lax.axis_index("tm"), lax.axis_index("dp")
    bits = bits_of(members)
    greet(me, size, members, bits, mine)

    to_after = remote(
        last_ref, before_ref, send_halo.at[0], recv_halo.at[0], {"tm": jnp.minimum(me + 1, size - 1)}
    )
    to_before = remote(
        first_ref, after_ref, send_halo.at[1], recv_halo.at[1], {"tm": jnp.maximum(me - 1, 0)}
    )

    @pl.when(me < size - 1)
    def _():
        to_after.start()

    @pl.when(me > 0)
    def _():
        to_before.start()

    outgoing = []
    for j in range(1, size):
        copy = remote(
            shard_ref.at[:, mine],
            full_ref.at[me, :, mine],
            send_tm.at[j],
            recv_tm.at[j],
            {"tm": lax.rem(me + j, size)},
        )
        copy.start()
        outgoing.append(copy)
    keep = pltpu.make_async_copy(shard_ref, full_ref.at[me], local_sem)
    keep.start()

    @pl.when(me == 0)
    def _():
        before_ref[...] = jnp.zeros_like(before_ref)

    @pl.when(me == size - 1)
    def _():
        after_ref[...] = jnp.zeros_like(after_ref)

    owned = [mine]
    number = 0
    for level, bit in enumerate(reversed(bits)):
        for j in range(1, size):
            source = lax.rem(me - j + size, size)
            if level == 0:
                remote(
                    shard_ref.at[:, mine],
                    full_ref.at[source, :, mine],
                    send_tm.at[j],
                    recv_tm.at[j],
                    {"tm": source},
                ).wait_recv()
            else:
                for copy in pending[j]:
                    copy.wait_recv()
            for place, quarter in enumerate(owned):
                copy = remote(
                    full_ref.at[source, :, quarter],
                    full_ref.at[source, :, quarter],
                    send_dp.at[number + place, j],
                    recv_dp.at[number + place, j],
                    {"dp": flip(mine, bit)},
                )
                copy.start()
                outgoing.append(copy)
        pending = {
            j: [
                remote(
                    full_ref.at[lax.rem(me - j + size, size), :, quarter],
                    full_ref.at[lax.rem(me - j + size, size), :, flip(quarter, bit)],
                    send_dp.at[number + place, j],
                    recv_dp.at[number + place, j],
                    {"dp": flip(mine, bit)},
                )
                for place, quarter in enumerate(owned)
            ]
            for j in range(1, size)
        }
        number += len(owned)
        owned = owned + [flip(quarter, bit) for quarter in owned]
    for j in range(1, size):
        for copy in pending[j]:
            copy.wait_recv()
    for copy in outgoing:
        copy.wait_send()
    keep.wait()

    @pl.when(me < size - 1)
    def _():
        to_after.wait_send()
        to_before.wait_recv()

    @pl.when(me > 0)
    def _():
        to_before.wait_send()
        to_after.wait_recv()


def gather_step(shard, first, last):
    size, members = lax.axis_size("tm"), lax.axis_size("dp")
    vmem = pl.BlockSpec(memory_space=pltpu.VMEM)
    dma = pltpu.SemaphoreType.DMA
    return pl.pallas_call(
        functools.partial(gather_kernel, size, members),
        out_shape=(
            jax.ShapeDtypeStruct((size,) + shard.shape, shard.dtype),
            jax.ShapeDtypeStruct(first.shape, first.dtype),
            jax.ShapeDtypeStruct(last.shape, last.dtype),
        ),
        in_specs=[vmem] * 3,
        out_specs=(vmem,) * 3,
        scratch_shapes=[
            dma((size,)), dma((size,)), dma((members, size)), dma((members, size)),
            dma((2,)), dma((2,)), dma,
        ],
        compiler_params=pltpu.CompilerParams(
            collective_id=0, has_side_effects=True, vmem_limit_bytes=32 * 1024 * 1024
        ),
    )(shard, first, last)


def reduce_kernel(
    size, members, grad_ref, square_ref, owned_ref, total_ref,
    halves, passed, crossed, kept, incoming, tiles, tile_in,
    send_core, recv_core, send_x, recv_x, send_tm, recv_tm, send_tile, recv_tile,
    send_gather, recv_gather, send_sum, recv_sum,
):
    me, mine = lax.axis_index("tm"), lax.axis_index("dp")
    bits = bits_of(members)
    near, far = bits
    partner, across = flip(mine, near), flip(mine, far)
    corner = flip(partner, far)
    greet(me, size, members, bits, mine)
    outgoing = []

    def begin(copy):
        copy.start()
        outgoing.append(copy)
        return copy

    order = list(range(1, size)) + [0]
    target = [lax.rem(me + j, size) for j in range(size)]
    core = {}
    for slot, quarter in ((1, corner), (0, partner)):
        for j in order:
            core[slot, j] = begin(
                remote(
                    grad_ref.at[target[j], :, quarter],
                    halves.at[slot, target[j]],
                    send_core.at[slot, j],
                    recv_core.at[slot, j],
                    {"dp": partner},
                )
            )
    x = {}
    for j in order:
        core[1, j].wait_recv()
        passed[target[j]] = (
            grad_ref[target[j], :, across].astype(jnp.float32)
            + halves[1, target[j]].astype(jnp.float32)
        ).astype(passed.dtype)
        x[j] = begin(
            remote(
                passed.at[target[j]], crossed.at[target[j]], send_x.at[j], recv_x.at[j],
                {"dp": across},
            )
        )
    for j in order:
        core[0, j].wait_recv()
        x[j].wait_recv()
        value = (
            grad_ref[target[j], :, mine].astype(jnp.float32)
            + halves[0, target[j]].astype(jnp.float32)
            + crossed[target[j]].astype(jnp.float32)
        )
        if j == 0:
            total = value
        else:
            kept[j] = value.astype(kept.dtype)
            begin(
                remote(
                    kept.at[j], incoming.at[j], send_tm.at[j], recv_tm.at[j], {"tm": target[j]}
                )
            )
    for j in range(1, size):
        source = lax.rem(me - j + size, size)
        remote(
            kept.at[j], incoming.at[j], send_tm.at[j], recv_tm.at[j], {"tm": source}
        ).wait_recv()
        total = total + incoming[j].astype(jnp.float32)
    rounded = total.astype(owned_ref.dtype)
    owned_ref[:, mine] = rounded

    def share(bit, quarter, number):
        return begin(
            remote(
                owned_ref.at[:, quarter], owned_ref.at[:, quarter], send_gather.at[number],
                recv_gather.at[number], {"dp": flip(mine, bit)},
            )
        )

    def take(bit, quarter, number):
        remote(
            owned_ref.at[:, flip(quarter, bit)], owned_ref.at[:, flip(quarter, bit)],
            send_gather.at[number], recv_gather.at[number], {"dp": flip(mine, bit)},
        ).wait_recv()

    back = rounded.astype(jnp.float32)
    powers = (back * back).reshape(-1, 8, back.shape[-1]).sum(axis=0)
    total_ref[...] = jnp.zeros_like(total_ref)
    width = powers.shape[-1]
    if width % 128 == 0:
        folded = powers[:, :128]
        for n in range(1, width // 128):
            folded = folded + powers[:, n * 128 : (n + 1) * 128]
        total_ref[8:16, :] = folded
    else:
        total_ref[8:16, :width] = powers
    total_ref[0:8, :] = square_ref[:, :128] + square_ref[:, 128:]
    tile_in[me] = total_ref[...]
    for j in range(1, size):
        begin(
            remote(
                total_ref, tile_in.at[me], send_tile.at[j], recv_tile.at[j], {"tm": target[j]}
            )
        )
    share(far, mine, 0)
    share(near, mine, 1)
    for j in range(1, size):
        source = lax.rem(me - j + size, size)
        remote(
            total_ref, tile_in.at[source], send_tile.at[j], recv_tile.at[j], {"tm": source}
        ).wait_recv()
    tiles[0] = tile_in[...].sum(axis=0)
    begin(remote(tiles.at[0], tiles.at[1], send_sum.at[0], recv_sum.at[0], {"dp": across}))
    take(far, mine, 0)
    share(near, across, 2)
    remote(tiles.at[0], tiles.at[1], send_sum.at[0], recv_sum.at[0], {"dp": across}).wait_recv()
    tiles[2] = tiles[0] + tiles[1]
    begin(remote(tiles.at[2], tiles.at[3], send_sum.at[1], recv_sum.at[1], {"dp": partner}))
    take(near, mine, 1)
    take(near, across, 2)
    remote(tiles.at[2], tiles.at[3], send_sum.at[1], recv_sum.at[1], {"dp": partner}).wait_recv()
    for copy in outgoing:
        copy.wait_send()
    total_ref[...] = tiles[2] + tiles[3]


def reduce_step(gradient, squares):
    size, parts, members, rows, width = gradient.shape
    assert members == 4
    vmem = pl.BlockSpec(memory_space=pltpu.VMEM)
    dma = pltpu.SemaphoreType.DMA
    piece = (parts, rows, width)
    kind = jnp.bfloat16
    return pl.pallas_call(
        functools.partial(reduce_kernel, size, members),
        out_shape=(
            jax.ShapeDtypeStruct((parts, members, rows, width), kind),
            jax.ShapeDtypeStruct((16, 128), jnp.float32),
        ),
        in_specs=[vmem] * 2,
        out_specs=(vmem,) * 2,
        scratch_shapes=[
            pltpu.VMEM((2, size) + piece, kind),
            pltpu.VMEM((size,) + piece, kind),
            pltpu.VMEM((size,) + piece, kind),
            pltpu.VMEM((size,) + piece, kind),
            pltpu.VMEM((size,) + piece, kind),
            pltpu.VMEM((4, 16, 128), jnp.float32),
            pltpu.VMEM((size, 16, 128), jnp.float32),
            dma((2, size)), dma((2, size)), dma((size,)), dma((size,)), dma((size,)),
            dma((size,)), dma((size,)), dma((size,)), dma((3,)), dma((3,)), dma((2,)), dma((2,)),
        ],
        compiler_params=pltpu.CompilerParams(
            collective_id=1, has_side_effects=True, vmem_limit_bytes=48 * 1024 * 1024
        ),
    )(gradient, squares)


def adam_direction(grad_part, square_total, entries, weight_part, first_part, second_part):
    rms_value = jnp.sqrt(square_total / entries + rms_eps)
    factor = jnp.minimum(1.0, 1.0 / rms_value)
    clipped = grad_part * factor
    first_new = beta_one * first_part + (1.0 - beta_one) * clipped
    second_new = beta_two * second_part + (1.0 - beta_two) * clipped * clipped
    first_hat = first_new / (1.0 - beta_one**step_count)
    second_hat = second_new / (1.0 - beta_two**step_count)
    return first_hat / (jnp.sqrt(second_hat) + adam_eps) + decay_rate * weight_part


def on_device(signal, weight, first_moment, second_moment, shuffle):
    windows, length, channels = signal.shape
    size, members = lax.axis_size("tm"), lax.axis_size("dp")
    depth, cols = weight.shape
    width = WIDE if cols % WIDE == 0 else cols
    parts, blocks = cols // width, channels // WIDE
    rows = depth // members
    shard = weight.astype(jnp.bfloat16).reshape(members, rows, parts, width).transpose(2, 0, 1, 3)
    first = signal[:, :HALO].reshape(windows * HALO, channels)
    last = signal[:, length - HALO :].reshape(windows * HALO, channels)
    full, before, after = gather_step(shard, first, last)
    full = (
        full.reshape(blocks, WIDE // width, depth, width)
        .transpose(0, 2, 1, 3)
        .reshape(blocks, depth, WIDE)
    )
    before = before.reshape(windows, HALO, channels)
    after = after.reshape(windows, HALO, channels)
    decoded, back_pre, gradient, squares = local_step(signal, full, shuffle, before, after)
    gradient = (
        gradient.reshape(blocks, depth, WIDE // width, width)
        .transpose(0, 2, 1, 3)
        .reshape(size, parts, members, rows, width)
    )
    owned, totals = reduce_step(gradient, squares)
    element_count = windows * members * length * size * channels
    mean_error = (jnp.sum(totals[:8]) / element_count).reshape(1)
    owned = owned.transpose(1, 2, 0, 3).reshape(depth, cols).astype(jnp.float32)
    square_total = jnp.sum(totals[8:])
    direction = adam_direction(owned, square_total, KW * CH, weight, first_moment, second_moment)
    return (decoded, mean_error, direction, back_pre)


def solution(mesh):
    return jax.shard_map(
        on_device,
        mesh=mesh,
        in_specs=(
            P(("parts", "dp"), "tm", None),
            P("parts", "tm"),
            P("parts", "tm"),
            P("parts", "tm"),
            P(),
        ),
        out_specs=(
            P(("parts", "dp"), "tm", None),
            P("parts"),
            P("parts", "tm"),
            P(("parts", "dp"), "tm", None),
        ),
        check_vma=False,
    )
```

```python
import functools

import jax
import jax.numpy as jnp
from jax import lax
from jax.experimental import pallas as pl
from jax.experimental.pallas import tpu as pltpu
from jax.sharding import PartitionSpec as P

GW = 64
KERNEL = 5
CH = 2048
KW = 320
WIDE = 256
HALO = 8

beta_one = 0.9
beta_two = 0.999
adam_eps = 1e-08
decay_rate = 0.1
rms_eps = 1e-06
step_count = 100

MESH = pl.DeviceIdType.MESH
TN = (((0,), (0,)), ((), ()))
NT = (((1,), (1,)), ((), ()))


def shifted(value, amount):
    rows = value.shape[0]
    return value if amount % rows == 0 else pltpu.roll(value, amount % rows, 0)


def local_part(value, windows, length):
    step = length + 2 * HALO
    return jnp.concatenate(
        [value[w * step + HALO : w * step + HALO + length] for w in range(windows)], axis=0
    )


def spread_part(value, windows, length):
    blank = jnp.zeros((HALO, value.shape[1]), value.dtype)
    pieces = []
    for w in range(windows):
        pieces += [blank, value[w * length : (w + 1) * length], blank]
    return jnp.concatenate(pieces, axis=0)


def diagonal(value):
    lane = lax.broadcasted_iota(jnp.int32, (GW, WIDE), 1) // GW
    picked = value[:GW]
    for j in range(1, WIDE // GW):
        picked = jnp.where(lane == j, value[j * GW : (j + 1) * GW], picked)
    return picked


def compute_kernel(
    windows, length, sig_ref, w_ref, shuffle_ref, rec_ref, back_ref, grad_ref, square_ref,
    onehot, table, pre, act, back, partial,
):
    channels = sig_ref.shape[1]
    blocks = channels // WIDE
    rows = sig_ref.shape[0]
    step = length + 2 * HALO
    me, peers = lax.axis_index("tm"), lax.axis_size("tm")
    place = lax.broadcasted_iota(jnp.int32, (rows, WIDE), 0)
    inner = lax.rem(place, step)
    low = jnp.where(me == 0, HALO, 0)
    high = jnp.where(me == peers - 1, HALO + length, step)
    inside = jnp.logical_and(inner >= low, inner < high)
    block_mask = (
        lax.broadcasted_iota(jnp.int32, (WIDE, WIDE), 0) // GW
        == lax.broadcasted_iota(jnp.int32, (WIDE, WIDE), 1) // GW
    )
    square_ref[...] = jnp.zeros_like(square_ref)

    def encode(index, carry):
        cols = pl.ds(pl.multiple_of(index * WIDE, WIDE), WIDE)
        for k in range(KERNEL):
            taps = w_ref[index, k * GW : (k + 1) * GW, :].astype(jnp.float32)
            tiled = jnp.concatenate([taps] * (WIDE // GW), axis=0)
            table[index, k * WIDE : (k + 1) * WIDE, :] = jnp.where(block_mask, tiled, 0.0).astype(
                jnp.bfloat16
            )
        x = sig_ref[:, cols].astype(jnp.float32)
        stack = jnp.concatenate(
            [shifted(x, 2 - k).astype(jnp.bfloat16) for k in range(KERNEL)], axis=1
        )
        value = jnp.dot(stack, table[index], preferred_element_type=jnp.float32)
        pre[:, cols] = local_part(value, windows, length)
        active = value / (1.0 + jnp.exp(-value))
        act[:, cols] = jnp.where(inside, active, 0.0).astype(jnp.bfloat16)
        return carry

    lax.fori_loop(0, blocks, encode, 0)

    def decode(index, carry):
        cols = pl.ds(pl.multiple_of(index * WIDE, WIDE), WIDE)
        source = lax.broadcasted_iota(jnp.int32, (channels, WIDE), 0)
        onehot[:, cols] = jnp.where(source == shuffle_ref[:, cols], 1.0, 0.0).astype(jnp.bfloat16)
        mixed = jnp.dot(act[...], onehot[:, cols], preferred_element_type=jnp.float32)
        decoded = jnp.zeros((rows, WIDE), jnp.float32)
        own_mixed = []
        for k in range(KERNEL):
            moved = shifted(mixed, k - 2)
            own_mixed.append(local_part(moved, windows, length).astype(jnp.bfloat16))
            decoded += lax.dot_general(
                moved.astype(jnp.bfloat16),
                table[index, k * WIDE : (k + 1) * WIDE, :],
                NT,
                preferred_element_type=jnp.float32,
            )
        error = jnp.where(inside, decoded - sig_ref[:, cols].astype(jnp.float32), 0.0)
        own_decoded = local_part(decoded, windows, length).astype(jnp.bfloat16)
        for w in range(windows):
            rec_ref[w, :, cols] = own_decoded[w * length : (w + 1) * length]
        own_error = local_part(error, windows, length)
        square_ref[...] += (own_error * own_error).reshape(-1, 8, WIDE).sum(axis=0)
        stack = jnp.concatenate(
            [shifted(error, 2 - k).astype(jnp.bfloat16) for k in range(KERNEL)], axis=1
        )
        value = jnp.dot(stack, table[index], preferred_element_type=jnp.float32)
        back[:, cols] = local_part(value, windows, length).astype(jnp.bfloat16)
        product = lax.dot_general(
            own_error.astype(jnp.bfloat16),
            jnp.concatenate(own_mixed, axis=1),
            TN,
            preferred_element_type=jnp.float32,
        )
        for k in range(KERNEL):
            partial[k * GW : (k + 1) * GW, cols] = diagonal(product[:, k * WIDE : (k + 1) * WIDE])
        return carry

    lax.fori_loop(0, blocks, decode, 0)

    def finish(index, carry):
        start = pl.multiple_of(index * WIDE, WIDE)
        cols = pl.ds(start, WIDE)
        restored = lax.dot_general(
            back[...], onehot[pl.ds(start, WIDE), :], NT, preferred_element_type=jnp.float32
        )
        value = pre[:, cols]
        sigma = 1.0 / (1.0 + jnp.exp(-value))
        own = (restored * (sigma * (1.0 + value * (1.0 - sigma)))).astype(jnp.bfloat16)
        for w in range(windows):
            back_ref[w, :, cols] = own[w * length : (w + 1) * length]
        wide = spread_part(own.astype(jnp.float32), windows, length)
        stack = jnp.concatenate(
            [shifted(wide, k - 2).astype(jnp.bfloat16) for k in range(KERNEL)], axis=1
        )
        product = lax.dot_general(
            sig_ref[:, cols], stack, TN, preferred_element_type=jnp.float32
        )
        for k in range(KERNEL):
            taken = slice(k * GW, (k + 1) * GW)
            total = partial[taken, cols] + diagonal(product[:, k * WIDE : (k + 1) * WIDE])
            grad_ref[index, taken, :] = total.astype(grad_ref.dtype)
        return carry

    lax.fori_loop(0, blocks, finish, 0)


def local_step(signal, weight, shuffle, before, after):
    windows, length, channels = signal.shape
    wide = jnp.concatenate([before, signal, after], axis=1)
    rows = windows * (length + 2 * HALO)
    vmem = pl.BlockSpec(memory_space=pltpu.VMEM)
    own = windows * length
    return pl.pallas_call(
        functools.partial(compute_kernel, windows, length),
        out_shape=(
            jax.ShapeDtypeStruct(signal.shape, jnp.bfloat16),
            jax.ShapeDtypeStruct(signal.shape, jnp.bfloat16),
            jax.ShapeDtypeStruct((channels // WIDE, KERNEL * GW, WIDE), jnp.bfloat16),
            jax.ShapeDtypeStruct((8, WIDE), jnp.float32),
        ),
        in_specs=[vmem] * 3,
        out_specs=(vmem,) * 4,
        scratch_shapes=[
            pltpu.VMEM((channels, channels), jnp.bfloat16),
            pltpu.VMEM((channels // WIDE, KERNEL * WIDE, WIDE), jnp.bfloat16),
            pltpu.VMEM((own, channels), jnp.float32),
            pltpu.VMEM((rows, channels), jnp.bfloat16),
            pltpu.VMEM((own, channels), jnp.bfloat16),
            pltpu.VMEM((KERNEL * GW, channels), jnp.float32),
        ],
        compiler_params=pltpu.CompilerParams(vmem_limit_bytes=48 * 1024 * 1024),
    )(wide.reshape(rows, channels), weight, shuffle.reshape(1, channels))


def flip(index, bit):
    return index + bit - 2 * bit * ((index // bit) % 2)


def bits_of(count):
    return [1 << b for b in range(count.bit_length() - 1)]


def greet(peers, size, members, bits, mine):
    barrier = pltpu.get_barrier_semaphore()
    for j in range(1, size):
        pl.semaphore_signal(
            barrier, inc=1, device_id={"tm": lax.rem(peers + j, size)}, device_id_type=MESH
        )
    for bit in bits:
        pl.semaphore_signal(
            barrier, inc=1, device_id={"dp": flip(mine, bit)}, device_id_type=MESH
        )
    pl.semaphore_wait(barrier, size - 1 + len(bits))


def remote(src, dst, send, recv, target):
    return pltpu.make_async_remote_copy(
        src_ref=src, dst_ref=dst, send_sem=send, recv_sem=recv, device_id=target,
        device_id_type=MESH,
    )


def gather_kernel(
    size, members, shard_ref, first_ref, last_ref, full_ref, before_ref, after_ref,
    send_tm, recv_tm, send_dp, recv_dp, send_halo, recv_halo, local_sem,
):
    me, mine = lax.axis_index("tm"), lax.axis_index("dp")
    bits = bits_of(members)
    greet(me, size, members, bits, mine)

    to_after = remote(
        last_ref, before_ref, send_halo.at[0], recv_halo.at[0], {"tm": jnp.minimum(me + 1, size - 1)}
    )
    to_before = remote(
        first_ref, after_ref, send_halo.at[1], recv_halo.at[1], {"tm": jnp.maximum(me - 1, 0)}
    )

    @pl.when(me < size - 1)
    def _():
        to_after.start()

    @pl.when(me > 0)
    def _():
        to_before.start()

    outgoing = []
    for j in range(1, size):
        copy = remote(
            shard_ref.at[:, mine],
            full_ref.at[me, :, mine],
            send_tm.at[j],
            recv_tm.at[j],
            {"tm": lax.rem(me + j, size)},
        )
        copy.start()
        outgoing.append(copy)
    keep = pltpu.make_async_copy(shard_ref, full_ref.at[me], local_sem)
    keep.start()

    @pl.when(me == 0)
    def _():
        before_ref[...] = jnp.zeros_like(before_ref)

    @pl.when(me == size - 1)
    def _():
        after_ref[...] = jnp.zeros_like(after_ref)

    owned = [mine]
    number = 0
    for level, bit in enumerate(reversed(bits)):
        for j in range(1, size):
            source = lax.rem(me - j + size, size)
            if level == 0:
                remote(
                    shard_ref.at[:, mine],
                    full_ref.at[source, :, mine],
                    send_tm.at[j],
                    recv_tm.at[j],
                    {"tm": source},
                ).wait_recv()
            else:
                for copy in pending[j]:
                    copy.wait_recv()
            for place, quarter in enumerate(owned):
                copy = remote(
                    full_ref.at[source, :, quarter],
                    full_ref.at[source, :, quarter],
                    send_dp.at[number + place, j],
                    recv_dp.at[number + place, j],
                    {"dp": flip(mine, bit)},
                )
                copy.start()
                outgoing.append(copy)
        pending = {
            j: [
                remote(
                    full_ref.at[lax.rem(me - j + size, size), :, quarter],
                    full_ref.at[lax.rem(me - j + size, size), :, flip(quarter, bit)],
                    send_dp.at[number + place, j],
                    recv_dp.at[number + place, j],
                    {"dp": flip(mine, bit)},
                )
                for place, quarter in enumerate(owned)
            ]
            for j in range(1, size)
        }
        number += len(owned)
        owned = owned + [flip(quarter, bit) for quarter in owned]
    for j in range(1, size):
        for copy in pending[j]:
            copy.wait_recv()
    for copy in outgoing:
        copy.wait_send()
    keep.wait()

    @pl.when(me < size - 1)
    def _():
        to_after.wait_send()
        to_before.wait_recv()

    @pl.when(me > 0)
    def _():
        to_before.wait_send()
        to_after.wait_recv()


def gather_step(shard, first, last):
    size, members = lax.axis_size("tm"), lax.axis_size("dp")
    vmem = pl.BlockSpec(memory_space=pltpu.VMEM)
    dma = pltpu.SemaphoreType.DMA
    return pl.pallas_call(
        functools.partial(gather_kernel, size, members),
        out_shape=(
            jax.ShapeDtypeStruct((size,) + shard.shape, shard.dtype),
            jax.ShapeDtypeStruct(first.shape, first.dtype),
            jax.ShapeDtypeStruct(last.shape, last.dtype),
        ),
        in_specs=[vmem] * 3,
        out_specs=(vmem,) * 3,
        scratch_shapes=[
            dma((size,)), dma((size,)), dma((members, size)), dma((members, size)),
            dma((2,)), dma((2,)), dma,
        ],
        compiler_params=pltpu.CompilerParams(
            collective_id=0, has_side_effects=True, vmem_limit_bytes=32 * 1024 * 1024
        ),
    )(shard, first, last)


def reduce_kernel(
    size, members, grad_ref, square_ref, owned_ref, total_ref,
    halves, passed, crossed, kept, incoming, tiles, tile_in,
    send_core, recv_core, send_x, recv_x, send_tm, recv_tm, send_tile, recv_tile,
    send_gather, recv_gather, send_sum, recv_sum,
):
    me, mine = lax.axis_index("tm"), lax.axis_index("dp")
    bits = bits_of(members)
    near, far = bits
    partner, across = flip(mine, near), flip(mine, far)
    corner = flip(partner, far)
    greet(me, size, members, bits, mine)
    outgoing = []

    def begin(copy):
        copy.start()
        outgoing.append(copy)
        return copy

    order = list(range(1, size)) + [0]
    target = [lax.rem(me + j, size) for j in range(size)]
    core = {}
    for slot, quarter in ((1, corner), (0, partner)):
        for j in order:
            core[slot, j] = begin(
                remote(
                    grad_ref.at[target[j], :, quarter],
                    halves.at[slot, target[j]],
                    send_core.at[slot, j],
                    recv_core.at[slot, j],
                    {"dp": partner},
                )
            )
    x = {}
    for j in order:
        core[1, j].wait_recv()
        passed[target[j]] = (
            grad_ref[target[j], :, across].astype(jnp.float32)
            + halves[1, target[j]].astype(jnp.float32)
        ).astype(passed.dtype)
        x[j] = begin(
            remote(
                passed.at[target[j]], crossed.at[target[j]], send_x.at[j], recv_x.at[j],
                {"dp": across},
            )
        )
    for j in order:
        core[0, j].wait_recv()
        x[j].wait_recv()
        value = (
            grad_ref[target[j], :, mine].astype(jnp.float32)
            + halves[0, target[j]].astype(jnp.float32)
            + crossed[target[j]].astype(jnp.float32)
        )
        if j == 0:
            total = value
        else:
            kept[j] = value.astype(kept.dtype)
            begin(
                remote(
                    kept.at[j], incoming.at[j], send_tm.at[j], recv_tm.at[j], {"tm": target[j]}
                )
            )
    for j in range(1, size):
        source = lax.rem(me - j + size, size)
        remote(
            kept.at[j], incoming.at[j], send_tm.at[j], recv_tm.at[j], {"tm": source}
        ).wait_recv()
        total = total + incoming[j].astype(jnp.float32)
    rounded = total.astype(owned_ref.dtype)
    owned_ref[:, mine] = rounded

    def share(bit, quarter, number):
        return begin(
            remote(
                owned_ref.at[:, quarter], owned_ref.at[:, quarter], send_gather.at[number],
                recv_gather.at[number], {"dp": flip(mine, bit)},
            )
        )

    def take(bit, quarter, number):
        remote(
            owned_ref.at[:, flip(quarter, bit)], owned_ref.at[:, flip(quarter, bit)],
            send_gather.at[number], recv_gather.at[number], {"dp": flip(mine, bit)},
        ).wait_recv()

    back = rounded.astype(jnp.float32)
    powers = (back * back).reshape(-1, 8, back.shape[-1]).sum(axis=0)
    total_ref[...] = jnp.zeros_like(total_ref)
    width = powers.shape[-1]
    if width % 128 == 0:
        folded = powers[:, :128]
        for n in range(1, width // 128):
            folded = folded + powers[:, n * 128 : (n + 1) * 128]
        total_ref[8:16, :] = folded
    else:
        total_ref[8:16, :width] = powers
    total_ref[0:8, :] = square_ref[:, :128] + square_ref[:, 128:]
    tile_in[me] = total_ref[...]
    for j in range(1, size):
        begin(
            remote(
                total_ref, tile_in.at[me], send_tile.at[j], recv_tile.at[j], {"tm": target[j]}
            )
        )
    share(far, mine, 0)
    share(near, mine, 1)
    for j in range(1, size):
        source = lax.rem(me - j + size, size)
        remote(
            total_ref, tile_in.at[source], send_tile.at[j], recv_tile.at[j], {"tm": source}
        ).wait_recv()
    tiles[0] = tile_in[...].sum(axis=0)
    begin(remote(tiles.at[0], tiles.at[1], send_sum.at[0], recv_sum.at[0], {"dp": across}))
    take(far, mine, 0)
    share(near, across, 2)
    remote(tiles.at[0], tiles.at[1], send_sum.at[0], recv_sum.at[0], {"dp": across}).wait_recv()
    tiles[2] = tiles[0] + tiles[1]
    begin(remote(tiles.at[2], tiles.at[3], send_sum.at[1], recv_sum.at[1], {"dp": partner}))
    take(near, mine, 1)
    take(near, across, 2)
    remote(tiles.at[2], tiles.at[3], send_sum.at[1], recv_sum.at[1], {"dp": partner}).wait_recv()
    for copy in outgoing:
        copy.wait_send()
    total_ref[...] = tiles[2] + tiles[3]


def reduce_step(gradient, squares):
    size, parts, members, rows, width = gradient.shape
    assert members == 4
    vmem = pl.BlockSpec(memory_space=pltpu.VMEM)
    dma = pltpu.SemaphoreType.DMA
    piece = (parts, rows, width)
    kind = jnp.bfloat16
    return pl.pallas_call(
        functools.partial(reduce_kernel, size, members),
        out_shape=(
            jax.ShapeDtypeStruct((parts, members, rows, width), kind),
            jax.ShapeDtypeStruct((16, 128), jnp.float32),
        ),
        in_specs=[vmem] * 2,
        out_specs=(vmem,) * 2,
        scratch_shapes=[
            pltpu.VMEM((2, size) + piece, kind),
            pltpu.VMEM((size,) + piece, kind),
            pltpu.VMEM((size,) + piece, kind),
            pltpu.VMEM((size,) + piece, kind),
            pltpu.VMEM((size,) + piece, kind),
            pltpu.VMEM((4, 16, 128), jnp.float32),
            pltpu.VMEM((size, 16, 128), jnp.float32),
            dma((2, size)), dma((2, size)), dma((size,)), dma((size,)), dma((size,)),
            dma((size,)), dma((size,)), dma((size,)), dma((3,)), dma((3,)), dma((2,)), dma((2,)),
        ],
        compiler_params=pltpu.CompilerParams(
            collective_id=1, has_side_effects=True, vmem_limit_bytes=48 * 1024 * 1024
        ),
    )(gradient, squares)


def fused_kernel(
    size, members, windows, length,
    signal_ref, weight_ref, shuffle_ref, rec_ref, back_ref, owned_ref, total_ref,
    onehot, table, pre, act, back, partial, wide, full, first, last, before, after,
    grad, square, halves, passed, crossed, kept, incoming, own_total, tiles, tile_in,
    send_halo, recv_halo, send_w, recv_w, send_f, recv_f,
    send_core, recv_core, send_x, recv_x, send_tm, recv_tm, send_tile, recv_tile,
    send_gather, recv_gather, send_sum, recv_sum,
):
    me, mine = lax.axis_index("tm"), lax.axis_index("dp")
    bits = bits_of(members)
    near, far = bits
    partner, across = flip(mine, near), flip(mine, far)
    corner = flip(partner, far)
    channels = signal_ref.shape[2]
    blocks = channels // WIDE
    parts = blocks // size
    quarter_rows = KERNEL * GW // members
    step = length + 2 * HALO
    rows = windows * step
    outgoing = []

    def begin(copy):
        copy.start()
        outgoing.append(copy)
        return copy

    for p in range(parts):
        for d in range(members):
            full[me, p, d] = weight_ref[
                d * quarter_rows : (d + 1) * quarter_rows, p * WIDE : (p + 1) * WIDE
            ].astype(full.dtype)
    first[...] = jnp.concatenate(
        [signal_ref[w, 0:16, :].astype(jnp.float32)[:HALO] for w in range(windows)], axis=0
    ).astype(first.dtype)
    last[...] = jnp.concatenate(
        [
            signal_ref[w, length - 16 : length, :].astype(jnp.float32)[16 - HALO :]
            for w in range(windows)
        ],
        axis=0,
    ).astype(last.dtype)

    greet(me, size, members, bits, mine)
    target = [lax.rem(me + j, size) for j in range(size)]
    source = [lax.rem(me - j + size, size) for j in range(size)]
    to_after = remote(
        last, before, send_halo.at[0], recv_halo.at[0], {"tm": jnp.minimum(me + 1, size - 1)}
    )
    to_before = remote(
        first, after, send_halo.at[1], recv_halo.at[1], {"tm": jnp.maximum(me - 1, 0)}
    )

    @pl.when(me < size - 1)
    def _():
        to_after.start()

    @pl.when(me > 0)
    def _():
        to_before.start()

    for j in range(1, size):
        begin(
            remote(
                full.at[me, :, mine], full.at[me, :, mine], send_w.at[j], recv_w.at[j],
                {"tm": target[j]},
            )
        )

    @pl.when(me == 0)
    def _():
        before[...] = jnp.zeros_like(before)

    @pl.when(me == size - 1)
    def _():
        after[...] = jnp.zeros_like(after)

    square[...] = jnp.zeros_like(square)

    def mark(index, carry):
        cols = pl.ds(pl.multiple_of(index * WIDE, WIDE), WIDE)
        row = lax.broadcasted_iota(jnp.int32, (channels, WIDE), 0)
        onehot[:, cols] = jnp.where(row == shuffle_ref[:, cols], 1.0, 0.0).astype(jnp.bfloat16)
        return carry

    lax.fori_loop(0, blocks, mark, 0)

    def weight_copy(origin, quarter, landed, level, j, where):
        return remote(
            full.at[origin, :, quarter], full.at[origin, :, landed], send_f.at[level, j],
            recv_f.at[level, j], {"dp": where},
        )

    for j in range(1, size):
        remote(
            full.at[me, :, mine], full.at[source[j], :, mine], send_w.at[j], recv_w.at[j],
            {"tm": source[j]},
        ).wait_recv()
        begin(weight_copy(source[j], mine, mine, 0, j, across))
        begin(weight_copy(source[j], mine, mine, 1, j, partner))

    @pl.when(me < size - 1)
    def _():
        to_after.wait_send()
        to_before.wait_recv()

    @pl.when(me > 0)
    def _():
        to_before.wait_send()
        to_after.wait_recv()

    place = lax.broadcasted_iota(jnp.int32, (rows, WIDE), 0)
    inner = lax.rem(place, step)
    low = jnp.where(me == 0, HALO, 0)
    high = jnp.where(me == size - 1, HALO + length, step)
    inside = jnp.logical_and(inner >= low, inner < high)
    block_mask = (
        lax.broadcasted_iota(jnp.int32, (WIDE, WIDE), 0) // GW
        == lax.broadcasted_iota(jnp.int32, (WIDE, WIDE), 1) // GW
    )

    def encode_from(origin):
        def encode(p, carry):
            index = origin * parts + p
            cols = pl.ds(pl.multiple_of(index * WIDE, WIDE), WIDE)
            weights = full[origin, p].astype(jnp.float32).reshape(KERNEL * GW, WIDE)
            for k in range(KERNEL):
                tiled = jnp.concatenate([weights[k * GW : (k + 1) * GW]] * (WIDE // GW), axis=0)
                table[index, k * WIDE : (k + 1) * WIDE, :] = jnp.where(
                    block_mask, tiled, 0.0
                ).astype(jnp.bfloat16)
            head = before[:, cols].astype(jnp.float32)
            tail = after[:, cols].astype(jnp.float32)
            pieces = []
            for w in range(windows):
                pieces += [
                    head[w * HALO : (w + 1) * HALO],
                    signal_ref[w, :, cols].astype(jnp.float32),
                    tail[w * HALO : (w + 1) * HALO],
                ]
            x = jnp.concatenate(pieces, axis=0)
            wide[:, cols] = x.astype(jnp.bfloat16)
            stack = jnp.concatenate(
                [shifted(x, 2 - k).astype(jnp.bfloat16) for k in range(KERNEL)], axis=1
            )
            value = jnp.dot(stack, table[index], preferred_element_type=jnp.float32)
            pre[:, cols] = local_part(value, windows, length)
            active = value / (1.0 + jnp.exp(-value))
            act[:, cols] = jnp.where(inside, active, 0.0).astype(jnp.bfloat16)
            return carry

        lax.fori_loop(0, parts, encode, 0)

    encode_from(me)
    for j in range(1, size):
        weight_copy(source[j], mine, across, 0, j, across).wait_recv()
        begin(weight_copy(source[j], across, across, 2, j, partner))
    for j in range(1, size):
        weight_copy(source[j], mine, partner, 1, j, partner).wait_recv()
        weight_copy(source[j], across, corner, 2, j, partner).wait_recv()
        encode_from(source[j])

    def decode(index, carry):
        cols = pl.ds(pl.multiple_of(index * WIDE, WIDE), WIDE)
        mixed = jnp.dot(act[...], onehot[:, cols], preferred_element_type=jnp.float32)
        decoded = jnp.zeros((rows, WIDE), jnp.float32)
        own_mixed = []
        for k in range(KERNEL):
            moved = shifted(mixed, k - 2)
            own_mixed.append(local_part(moved, windows, length).astype(jnp.bfloat16))
            decoded += lax.dot_general(
                moved.astype(jnp.bfloat16),
                table[index, k * WIDE : (k + 1) * WIDE, :],
                NT,
                preferred_element_type=jnp.float32,
            )
        error = jnp.where(inside, decoded - wide[:, cols].astype(jnp.float32), 0.0)
        own_decoded = local_part(decoded, windows, length).astype(jnp.bfloat16)
        for w in range(windows):
            rec_ref[w, :, cols] = own_decoded[w * length : (w + 1) * length]
        own_error = local_part(error, windows, length)
        square[...] += (own_error * own_error).reshape(-1, 8, WIDE).sum(axis=0)
        stack = jnp.concatenate(
            [shifted(error, 2 - k).astype(jnp.bfloat16) for k in range(KERNEL)], axis=1
        )
        value = jnp.dot(stack, table[index], preferred_element_type=jnp.float32)
        back[:, cols] = local_part(value, windows, length).astype(jnp.bfloat16)
        product = lax.dot_general(
            own_error.astype(jnp.bfloat16),
            jnp.concatenate(own_mixed, axis=1),
            TN,
            preferred_element_type=jnp.float32,
        )
        for k in range(KERNEL):
            partial[index, k * GW : (k + 1) * GW, :] = diagonal(
                product[:, k * WIDE : (k + 1) * WIDE]
            )
        return carry

    lax.fori_loop(0, blocks, decode, 0)

    def finish_for(owner):
        def finish(p, carry):
            index = owner * parts + p
            start = pl.multiple_of(index * WIDE, WIDE)
            cols = pl.ds(start, WIDE)
            restored = lax.dot_general(
                back[...], onehot[pl.ds(start, WIDE), :], NT, preferred_element_type=jnp.float32
            )
            value = pre[:, cols]
            sigma = 1.0 / (1.0 + jnp.exp(-value))
            own = (restored * (sigma * (1.0 + value * (1.0 - sigma)))).astype(jnp.bfloat16)
            for w in range(windows):
                back_ref[w, :, cols] = own[w * length : (w + 1) * length]
            spread = spread_part(own.astype(jnp.float32), windows, length)
            stack = jnp.concatenate(
                [shifted(spread, k - 2).astype(jnp.bfloat16) for k in range(KERNEL)], axis=1
            )
            product = lax.dot_general(wide[:, cols], stack, TN, preferred_element_type=jnp.float32)
            total = partial[index] + jnp.concatenate(
                [diagonal(product[:, k * WIDE : (k + 1) * WIDE]) for k in range(KERNEL)], axis=0
            )
            grad[owner, p] = total.reshape(members, quarter_rows, WIDE).astype(grad.dtype)
            return carry

        lax.fori_loop(0, parts, finish, 0)

    core, x = {}, {}

    def send_core_chunk(j):
        for slot, quarter in ((1, corner), (0, partner)):
            core[slot, j] = begin(
                remote(
                    grad.at[target[j], :, quarter], halves.at[slot, j], send_core.at[slot, j],
                    recv_core.at[slot, j], {"dp": partner},
                )
            )

    def send_x_chunk(j):
        core[1, j].wait_recv()
        passed[j] = (
            grad[target[j], :, across].astype(jnp.float32) + halves[1, j].astype(jnp.float32)
        ).astype(passed.dtype)
        x[j] = begin(
            remote(passed.at[j], crossed.at[j], send_x.at[j], recv_x.at[j], {"dp": across})
        )

    def send_tm_chunk(j):
        core[0, j].wait_recv()
        x[j].wait_recv()
        value = (
            grad[target[j], :, mine].astype(jnp.float32)
            + halves[0, j].astype(jnp.float32)
            + crossed[j].astype(jnp.float32)
        )
        if j == 0:
            own_total[...] = value
        else:
            kept[j] = value.astype(kept.dtype)
            begin(
                remote(
                    kept.at[j], incoming.at[j], send_tm.at[j], recv_tm.at[j], {"tm": target[j]}
                )
            )

    order = list(range(1, size)) + [0]
    for n in range(size + 2):
        if n < size:
            finish_for(target[order[n]])
            send_core_chunk(order[n])
        if 1 <= n <= size:
            send_x_chunk(order[n - 1])
        if n >= 2:
            send_tm_chunk(order[n - 2])

    total = own_total[...]
    for j in range(1, size):
        remote(
            kept.at[j], incoming.at[j], send_tm.at[j], recv_tm.at[j], {"tm": source[j]}
        ).wait_recv()
        total = total + incoming[j].astype(jnp.float32)
    rounded = total.astype(owned_ref.dtype)
    owned_ref[:, mine] = rounded

    def share(bit, quarter, number):
        return begin(
            remote(
                owned_ref.at[:, quarter], owned_ref.at[:, quarter], send_gather.at[number],
                recv_gather.at[number], {"dp": flip(mine, bit)},
            )
        )

    def take(bit, quarter, number):
        remote(
            owned_ref.at[:, flip(quarter, bit)], owned_ref.at[:, flip(quarter, bit)],
            send_gather.at[number], recv_gather.at[number], {"dp": flip(mine, bit)},
        ).wait_recv()

    back = rounded.astype(jnp.float32)
    powers = (back * back).reshape(-1, 8, back.shape[-1]).sum(axis=0)
    total_ref[...] = jnp.zeros_like(total_ref)
    width = powers.shape[-1]
    if width % 128 == 0:
        folded = powers[:, :128]
        for n in range(1, width // 128):
            folded = folded + powers[:, n * 128 : (n + 1) * 128]
        total_ref[8:16, :] = folded
    else:
        total_ref[8:16, :width] = powers
    total_ref[0:8, :] = square[:, :128] + square[:, 128:]
    tile_in[me] = total_ref[...]
    for j in range(1, size):
        begin(
            remote(
                total_ref, tile_in.at[me], send_tile.at[j], recv_tile.at[j], {"tm": target[j]}
            )
        )
    share(far, mine, 0)
    share(near, mine, 1)
    for j in range(1, size):
        remote(
            total_ref, tile_in.at[source[j]], send_tile.at[j], recv_tile.at[j], {"tm": source[j]}
        ).wait_recv()
    tiles[0] = tile_in[...].sum(axis=0)
    begin(remote(tiles.at[0], tiles.at[1], send_sum.at[0], recv_sum.at[0], {"dp": across}))
    take(far, mine, 0)
    share(near, across, 2)
    remote(tiles.at[0], tiles.at[1], send_sum.at[0], recv_sum.at[0], {"dp": across}).wait_recv()
    tiles[2] = tiles[0] + tiles[1]
    begin(remote(tiles.at[2], tiles.at[3], send_sum.at[1], recv_sum.at[1], {"dp": partner}))
    take(near, mine, 1)
    take(near, across, 2)
    remote(tiles.at[2], tiles.at[3], send_sum.at[1], recv_sum.at[1], {"dp": partner}).wait_recv()
    for copy in outgoing:
        copy.wait_send()
    total_ref[...] = tiles[2] + tiles[3]


def fused_step(signal, weight, shuffle):
    size, members = lax.axis_size("tm"), lax.axis_size("dp")
    assert members == 4
    windows, length, channels = signal.shape
    depth, cols = weight.shape
    parts, blocks, quarter = cols // WIDE, channels // WIDE, depth // members
    own, rows = windows * length, windows * (length + 2 * HALO)
    vmem = pl.BlockSpec(memory_space=pltpu.VMEM)
    dma = pltpu.SemaphoreType.DMA
    kind = jnp.bfloat16
    piece = (parts, quarter, WIDE)
    everything = (size, parts, members, quarter, WIDE)
    edge = pltpu.VMEM((windows * HALO, channels), kind)
    return pl.pallas_call(
        functools.partial(fused_kernel, size, members, windows, length),
        out_shape=(
            jax.ShapeDtypeStruct(signal.shape, kind),
            jax.ShapeDtypeStruct(signal.shape, kind),
            jax.ShapeDtypeStruct((parts, members, quarter, WIDE), kind),
            jax.ShapeDtypeStruct((16, 128), jnp.float32),
        ),
        in_specs=[vmem] * 3,
        out_specs=(vmem,) * 4,
        scratch_shapes=[
            pltpu.VMEM((channels, channels), kind),
            pltpu.VMEM((blocks, KERNEL * WIDE, WIDE), kind),
            pltpu.VMEM((own, channels), jnp.float32),
            pltpu.VMEM((rows, channels), kind),
            pltpu.VMEM((own, channels), kind),
            pltpu.VMEM((blocks, depth, WIDE), jnp.float32),
            pltpu.VMEM((rows, channels), kind),
            pltpu.VMEM(everything, kind),
            edge, edge, edge, edge,
            pltpu.VMEM(everything, kind),
            pltpu.VMEM((8, WIDE), jnp.float32),
            pltpu.VMEM((2, size) + piece, kind),
            pltpu.VMEM((size,) + piece, kind),
            pltpu.VMEM((size,) + piece, kind),
            pltpu.VMEM((size,) + piece, kind),
            pltpu.VMEM((size,) + piece, kind),
            pltpu.VMEM(piece, jnp.float32),
            pltpu.VMEM((4, 16, 128), jnp.float32),
            pltpu.VMEM((size, 16, 128), jnp.float32),
            dma((2,)), dma((2,)), dma((size,)), dma((size,)), dma((3, size)), dma((3, size)),
            dma((2, size)), dma((2, size)), dma((size,)), dma((size,)), dma((size,)),
            dma((size,)), dma((size,)), dma((size,)), dma((3,)), dma((3,)), dma((2,)), dma((2,)),
        ],
        compiler_params=pltpu.CompilerParams(
            collective_id=2, has_side_effects=True, vmem_limit_bytes=56 * 1024 * 1024
        ),
    )(signal, weight, shuffle.reshape(1, channels))


def adam_direction(grad_part, square_total, entries, weight_part, first_part, second_part):
    rms_value = jnp.sqrt(square_total / entries + rms_eps)
    factor = jnp.minimum(1.0, 1.0 / rms_value)
    clipped = grad_part * factor
    first_new = beta_one * first_part + (1.0 - beta_one) * clipped
    second_new = beta_two * second_part + (1.0 - beta_two) * clipped * clipped
    first_hat = first_new / (1.0 - beta_one**step_count)
    second_hat = second_new / (1.0 - beta_two**step_count)
    return first_hat / (jnp.sqrt(second_hat) + adam_eps) + decay_rate * weight_part


def on_device(signal, weight, first_moment, second_moment, shuffle):
    windows, length, channels = signal.shape
    size, members = lax.axis_size("tm"), lax.axis_size("dp")
    depth, cols = weight.shape
    width = WIDE if cols % WIDE == 0 else cols
    parts, blocks = cols // width, channels // WIDE
    rows = depth // members
    if cols % WIDE == 0:
        decoded, back_pre, owned, totals = fused_step(signal, weight, shuffle)
    else:
        shard = weight.astype(jnp.bfloat16).reshape(members, rows, parts, width).transpose(2, 0, 1, 3)
        first = signal[:, :HALO].reshape(windows * HALO, channels)
        last = signal[:, length - HALO :].reshape(windows * HALO, channels)
        full, before, after = gather_step(shard, first, last)
        full = (
            full.reshape(blocks, WIDE // width, depth, width)
            .transpose(0, 2, 1, 3)
            .reshape(blocks, depth, WIDE)
        )
        before = before.reshape(windows, HALO, channels)
        after = after.reshape(windows, HALO, channels)
        decoded, back_pre, gradient, squares = local_step(signal, full, shuffle, before, after)
        gradient = (
            gradient.reshape(blocks, depth, WIDE // width, width)
            .transpose(0, 2, 1, 3)
            .reshape(size, parts, members, rows, width)
        )
        owned, totals = reduce_step(gradient, squares)
    element_count = windows * members * length * size * channels
    mean_error = (jnp.sum(totals[:8]) / element_count).reshape(1)
    owned = owned.transpose(1, 2, 0, 3).reshape(depth, cols).astype(jnp.float32)
    square_total = jnp.sum(totals[8:])
    direction = adam_direction(owned, square_total, KW * CH, weight, first_moment, second_moment)
    return (decoded, mean_error, direction, back_pre)


def solution(mesh):
    return jax.shard_map(
        on_device,
        mesh=mesh,
        in_specs=(
            P(("parts", "dp"), "tm", None),
            P("parts", "tm"),
            P("parts", "tm"),
            P("parts", "tm"),
            P(),
        ),
        out_specs=(
            P(("parts", "dp"), "tm", None),
            P("parts"),
            P("parts", "tm"),
            P(("parts", "dp"), "tm", None),
        ),
        check_vma=False,
    )
```

```python
import functools

import jax
import jax.numpy as jnp
from jax import lax
from jax.experimental import pallas as pl
from jax.experimental.pallas import tpu as pltpu
from jax.sharding import PartitionSpec as P

GW = 64
KERNEL = 5
CH = 2048
KW = 320
WIDE = 256
HALO = 8

beta_one = 0.9
beta_two = 0.999
adam_eps = 1e-08
decay_rate = 0.1
rms_eps = 1e-06
step_count = 100

MESH = pl.DeviceIdType.MESH
TN = (((0,), (0,)), ((), ()))
NT = (((1,), (1,)), ((), ()))


def shifted(value, amount):
    rows = value.shape[0]
    return value if amount % rows == 0 else pltpu.roll(value, amount % rows, 0)


def local_part(value, windows, length):
    step = length + 2 * HALO
    return jnp.concatenate(
        [value[w * step + HALO : w * step + HALO + length] for w in range(windows)], axis=0
    )


def spread_part(value, windows, length):
    blank = jnp.zeros((HALO, value.shape[1]), value.dtype)
    pieces = []
    for w in range(windows):
        pieces += [blank, value[w * length : (w + 1) * length], blank]
    return jnp.concatenate(pieces, axis=0)


def diagonal(value):
    lane = lax.broadcasted_iota(jnp.int32, (GW, WIDE), 1) // GW
    picked = value[:GW]
    for j in range(1, WIDE // GW):
        picked = jnp.where(lane == j, value[j * GW : (j + 1) * GW], picked)
    return picked


def compute_kernel(
    windows, length, sig_ref, w_ref, shuffle_ref, rec_ref, back_ref, grad_ref, square_ref,
    onehot, table, pre, act, back, partial,
):
    channels = sig_ref.shape[1]
    blocks = channels // WIDE
    rows = sig_ref.shape[0]
    step = length + 2 * HALO
    me, peers = lax.axis_index("tm"), lax.axis_size("tm")
    place = lax.broadcasted_iota(jnp.int32, (rows, WIDE), 0)
    inner = lax.rem(place, step)
    low = jnp.where(me == 0, HALO, 0)
    high = jnp.where(me == peers - 1, HALO + length, step)
    inside = jnp.logical_and(inner >= low, inner < high)
    block_mask = (
        lax.broadcasted_iota(jnp.int32, (WIDE, WIDE), 0) // GW
        == lax.broadcasted_iota(jnp.int32, (WIDE, WIDE), 1) // GW
    )
    square_ref[...] = jnp.zeros_like(square_ref)

    def encode(index, carry):
        cols = pl.ds(pl.multiple_of(index * WIDE, WIDE), WIDE)
        for k in range(KERNEL):
            taps = w_ref[index, k * GW : (k + 1) * GW, :].astype(jnp.float32)
            tiled = jnp.concatenate([taps] * (WIDE // GW), axis=0)
            table[index, k * WIDE : (k + 1) * WIDE, :] = jnp.where(block_mask, tiled, 0.0).astype(
                jnp.bfloat16
            )
        x = sig_ref[:, cols].astype(jnp.float32)
        stack = jnp.concatenate(
            [shifted(x, 2 - k).astype(jnp.bfloat16) for k in range(KERNEL)], axis=1
        )
        value = jnp.dot(stack, table[index], preferred_element_type=jnp.float32)
        pre[:, cols] = local_part(value, windows, length)
        active = value / (1.0 + jnp.exp(-value))
        act[:, cols] = jnp.where(inside, active, 0.0).astype(jnp.bfloat16)
        return carry

    lax.fori_loop(0, blocks, encode, 0)

    def decode(index, carry):
        cols = pl.ds(pl.multiple_of(index * WIDE, WIDE), WIDE)
        source = lax.broadcasted_iota(jnp.int32, (channels, WIDE), 0)
        onehot[:, cols] = jnp.where(source == shuffle_ref[:, cols], 1.0, 0.0).astype(jnp.bfloat16)
        mixed = jnp.dot(act[...], onehot[:, cols], preferred_element_type=jnp.float32)
        decoded = jnp.zeros((rows, WIDE), jnp.float32)
        own_mixed = []
        for k in range(KERNEL):
            moved = shifted(mixed, k - 2)
            own_mixed.append(local_part(moved, windows, length).astype(jnp.bfloat16))
            decoded += lax.dot_general(
                moved.astype(jnp.bfloat16),
                table[index, k * WIDE : (k + 1) * WIDE, :],
                NT,
                preferred_element_type=jnp.float32,
            )
        error = jnp.where(inside, decoded - sig_ref[:, cols].astype(jnp.float32), 0.0)
        own_decoded = local_part(decoded, windows, length).astype(jnp.bfloat16)
        for w in range(windows):
            rec_ref[w, :, cols] = own_decoded[w * length : (w + 1) * length]
        own_error = local_part(error, windows, length)
        square_ref[...] += (own_error * own_error).reshape(-1, 8, WIDE).sum(axis=0)
        stack = jnp.concatenate(
            [shifted(error, 2 - k).astype(jnp.bfloat16) for k in range(KERNEL)], axis=1
        )
        value = jnp.dot(stack, table[index], preferred_element_type=jnp.float32)
        back[:, cols] = local_part(value, windows, length).astype(jnp.bfloat16)
        product = lax.dot_general(
            own_error.astype(jnp.bfloat16),
            jnp.concatenate(own_mixed, axis=1),
            TN,
            preferred_element_type=jnp.float32,
        )
        for k in range(KERNEL):
            partial[k * GW : (k + 1) * GW, cols] = diagonal(product[:, k * WIDE : (k + 1) * WIDE])
        return carry

    lax.fori_loop(0, blocks, decode, 0)

    def finish(index, carry):
        start = pl.multiple_of(index * WIDE, WIDE)
        cols = pl.ds(start, WIDE)
        restored = lax.dot_general(
            back[...], onehot[pl.ds(start, WIDE), :], NT, preferred_element_type=jnp.float32
        )
        value = pre[:, cols]
        sigma = 1.0 / (1.0 + jnp.exp(-value))
        own = (restored * (sigma * (1.0 + value * (1.0 - sigma)))).astype(jnp.bfloat16)
        for w in range(windows):
            back_ref[w, :, cols] = own[w * length : (w + 1) * length]
        wide = spread_part(own.astype(jnp.float32), windows, length)
        stack = jnp.concatenate(
            [shifted(wide, k - 2).astype(jnp.bfloat16) for k in range(KERNEL)], axis=1
        )
        product = lax.dot_general(
            sig_ref[:, cols], stack, TN, preferred_element_type=jnp.float32
        )
        for k in range(KERNEL):
            taken = slice(k * GW, (k + 1) * GW)
            total = partial[taken, cols] + diagonal(product[:, k * WIDE : (k + 1) * WIDE])
            grad_ref[index, taken, :] = total.astype(grad_ref.dtype)
        return carry

    lax.fori_loop(0, blocks, finish, 0)


def local_step(signal, weight, shuffle, before, after):
    windows, length, channels = signal.shape
    wide = jnp.concatenate([before, signal, after], axis=1)
    rows = windows * (length + 2 * HALO)
    vmem = pl.BlockSpec(memory_space=pltpu.VMEM)
    own = windows * length
    return pl.pallas_call(
        functools.partial(compute_kernel, windows, length),
        out_shape=(
            jax.ShapeDtypeStruct(signal.shape, jnp.bfloat16),
            jax.ShapeDtypeStruct(signal.shape, jnp.bfloat16),
            jax.ShapeDtypeStruct((channels // WIDE, KERNEL * GW, WIDE), jnp.bfloat16),
            jax.ShapeDtypeStruct((8, WIDE), jnp.float32),
        ),
        in_specs=[vmem] * 3,
        out_specs=(vmem,) * 4,
        scratch_shapes=[
            pltpu.VMEM((channels, channels), jnp.bfloat16),
            pltpu.VMEM((channels // WIDE, KERNEL * WIDE, WIDE), jnp.bfloat16),
            pltpu.VMEM((own, channels), jnp.float32),
            pltpu.VMEM((rows, channels), jnp.bfloat16),
            pltpu.VMEM((own, channels), jnp.bfloat16),
            pltpu.VMEM((KERNEL * GW, channels), jnp.float32),
        ],
        compiler_params=pltpu.CompilerParams(vmem_limit_bytes=48 * 1024 * 1024),
    )(wide.reshape(rows, channels), weight, shuffle.reshape(1, channels))


def flip(index, bit):
    return index + bit - 2 * bit * ((index // bit) % 2)


def bits_of(count):
    return [1 << b for b in range(count.bit_length() - 1)]


def greet(peers, size, members, bits, mine):
    barrier = pltpu.get_barrier_semaphore()
    for j in range(1, size):
        pl.semaphore_signal(
            barrier, inc=1, device_id={"tm": lax.rem(peers + j, size)}, device_id_type=MESH
        )
    for bit in bits:
        pl.semaphore_signal(
            barrier, inc=1, device_id={"dp": flip(mine, bit)}, device_id_type=MESH
        )
    pl.semaphore_wait(barrier, size - 1 + len(bits))


def remote(src, dst, send, recv, target):
    return pltpu.make_async_remote_copy(
        src_ref=src, dst_ref=dst, send_sem=send, recv_sem=recv, device_id=target,
        device_id_type=MESH,
    )


def gather_kernel(
    size, members, shard_ref, first_ref, last_ref, full_ref, before_ref, after_ref,
    send_tm, recv_tm, send_dp, recv_dp, send_halo, recv_halo, local_sem,
):
    me, mine = lax.axis_index("tm"), lax.axis_index("dp")
    bits = bits_of(members)
    greet(me, size, members, bits, mine)

    to_after = remote(
        last_ref, before_ref, send_halo.at[0], recv_halo.at[0], {"tm": jnp.minimum(me + 1, size - 1)}
    )
    to_before = remote(
        first_ref, after_ref, send_halo.at[1], recv_halo.at[1], {"tm": jnp.maximum(me - 1, 0)}
    )

    @pl.when(me < size - 1)
    def _():
        to_after.start()

    @pl.when(me > 0)
    def _():
        to_before.start()

    outgoing = []
    for j in range(1, size):
        copy = remote(
            shard_ref.at[:, mine],
            full_ref.at[me, :, mine],
            send_tm.at[j],
            recv_tm.at[j],
            {"tm": lax.rem(me + j, size)},
        )
        copy.start()
        outgoing.append(copy)
    keep = pltpu.make_async_copy(shard_ref, full_ref.at[me], local_sem)
    keep.start()

    @pl.when(me == 0)
    def _():
        before_ref[...] = jnp.zeros_like(before_ref)

    @pl.when(me == size - 1)
    def _():
        after_ref[...] = jnp.zeros_like(after_ref)

    owned = [mine]
    number = 0
    for level, bit in enumerate(reversed(bits)):
        for j in range(1, size):
            source = lax.rem(me - j + size, size)
            if level == 0:
                remote(
                    shard_ref.at[:, mine],
                    full_ref.at[source, :, mine],
                    send_tm.at[j],
                    recv_tm.at[j],
                    {"tm": source},
                ).wait_recv()
            else:
                for copy in pending[j]:
                    copy.wait_recv()
            for place, quarter in enumerate(owned):
                copy = remote(
                    full_ref.at[source, :, quarter],
                    full_ref.at[source, :, quarter],
                    send_dp.at[number + place, j],
                    recv_dp.at[number + place, j],
                    {"dp": flip(mine, bit)},
                )
                copy.start()
                outgoing.append(copy)
        pending = {
            j: [
                remote(
                    full_ref.at[lax.rem(me - j + size, size), :, quarter],
                    full_ref.at[lax.rem(me - j + size, size), :, flip(quarter, bit)],
                    send_dp.at[number + place, j],
                    recv_dp.at[number + place, j],
                    {"dp": flip(mine, bit)},
                )
                for place, quarter in enumerate(owned)
            ]
            for j in range(1, size)
        }
        number += len(owned)
        owned = owned + [flip(quarter, bit) for quarter in owned]
    for j in range(1, size):
        for copy in pending[j]:
            copy.wait_recv()
    for copy in outgoing:
        copy.wait_send()
    keep.wait()

    @pl.when(me < size - 1)
    def _():
        to_after.wait_send()
        to_before.wait_recv()

    @pl.when(me > 0)
    def _():
        to_before.wait_send()
        to_after.wait_recv()


def gather_step(shard, first, last):
    size, members = lax.axis_size("tm"), lax.axis_size("dp")
    vmem = pl.BlockSpec(memory_space=pltpu.VMEM)
    dma = pltpu.SemaphoreType.DMA
    return pl.pallas_call(
        functools.partial(gather_kernel, size, members),
        out_shape=(
            jax.ShapeDtypeStruct((size,) + shard.shape, shard.dtype),
            jax.ShapeDtypeStruct(first.shape, first.dtype),
            jax.ShapeDtypeStruct(last.shape, last.dtype),
        ),
        in_specs=[vmem] * 3,
        out_specs=(vmem,) * 3,
        scratch_shapes=[
            dma((size,)), dma((size,)), dma((members, size)), dma((members, size)),
            dma((2,)), dma((2,)), dma,
        ],
        compiler_params=pltpu.CompilerParams(
            collective_id=0, has_side_effects=True, vmem_limit_bytes=32 * 1024 * 1024
        ),
    )(shard, first, last)


def reduce_kernel(
    size, members, grad_ref, square_ref, owned_ref, total_ref,
    halves, passed, crossed, kept, incoming, tiles, tile_in,
    send_core, recv_core, send_x, recv_x, send_tm, recv_tm, send_tile, recv_tile,
    send_gather, recv_gather, send_sum, recv_sum,
):
    me, mine = lax.axis_index("tm"), lax.axis_index("dp")
    bits = bits_of(members)
    near, far = bits
    partner, across = flip(mine, near), flip(mine, far)
    corner = flip(partner, far)
    greet(me, size, members, bits, mine)
    outgoing = []

    def begin(copy):
        copy.start()
        outgoing.append(copy)
        return copy

    order = list(range(1, size)) + [0]
    target = [lax.rem(me + j, size) for j in range(size)]
    core = {}
    for slot, quarter in ((1, corner), (0, partner)):
        for j in order:
            core[slot, j] = begin(
                remote(
                    grad_ref.at[target[j], :, quarter],
                    halves.at[slot, target[j]],
                    send_core.at[slot, j],
                    recv_core.at[slot, j],
                    {"dp": partner},
                )
            )
    x = {}
    for j in order:
        core[1, j].wait_recv()
        passed[target[j]] = (
            grad_ref[target[j], :, across].astype(jnp.float32)
            + halves[1, target[j]].astype(jnp.float32)
        ).astype(passed.dtype)
        x[j] = begin(
            remote(
                passed.at[target[j]], crossed.at[target[j]], send_x.at[j], recv_x.at[j],
                {"dp": across},
            )
        )
    for j in order:
        core[0, j].wait_recv()
        x[j].wait_recv()
        value = (
            grad_ref[target[j], :, mine].astype(jnp.float32)
            + halves[0, target[j]].astype(jnp.float32)
            + crossed[target[j]].astype(jnp.float32)
        )
        if j == 0:
            total = value
        else:
            kept[j] = value.astype(kept.dtype)
            begin(
                remote(
                    kept.at[j], incoming.at[j], send_tm.at[j], recv_tm.at[j], {"tm": target[j]}
                )
            )
    for j in range(1, size):
        source = lax.rem(me - j + size, size)
        remote(
            kept.at[j], incoming.at[j], send_tm.at[j], recv_tm.at[j], {"tm": source}
        ).wait_recv()
        total = total + incoming[j].astype(jnp.float32)
    rounded = total.astype(owned_ref.dtype)
    owned_ref[:, mine] = rounded

    def share(bit, quarter, number):
        return begin(
            remote(
                owned_ref.at[:, quarter], owned_ref.at[:, quarter], send_gather.at[number],
                recv_gather.at[number], {"dp": flip(mine, bit)},
            )
        )

    def take(bit, quarter, number):
        remote(
            owned_ref.at[:, flip(quarter, bit)], owned_ref.at[:, flip(quarter, bit)],
            send_gather.at[number], recv_gather.at[number], {"dp": flip(mine, bit)},
        ).wait_recv()

    back = rounded.astype(jnp.float32)
    powers = (back * back).reshape(-1, 8, back.shape[-1]).sum(axis=0)
    total_ref[...] = jnp.zeros_like(total_ref)
    width = powers.shape[-1]
    if width % 128 == 0:
        folded = powers[:, :128]
        for n in range(1, width // 128):
            folded = folded + powers[:, n * 128 : (n + 1) * 128]
        total_ref[8:16, :] = folded
    else:
        total_ref[8:16, :width] = powers
    total_ref[0:8, :] = square_ref[:, :128] + square_ref[:, 128:]
    tile_in[me] = total_ref[...]
    for j in range(1, size):
        begin(
            remote(
                total_ref, tile_in.at[me], send_tile.at[j], recv_tile.at[j], {"tm": target[j]}
            )
        )
    share(far, mine, 0)
    share(near, mine, 1)
    for j in range(1, size):
        source = lax.rem(me - j + size, size)
        remote(
            total_ref, tile_in.at[source], send_tile.at[j], recv_tile.at[j], {"tm": source}
        ).wait_recv()
    tiles[0] = tile_in[...].sum(axis=0)
    begin(remote(tiles.at[0], tiles.at[1], send_sum.at[0], recv_sum.at[0], {"dp": across}))
    take(far, mine, 0)
    share(near, across, 2)
    remote(tiles.at[0], tiles.at[1], send_sum.at[0], recv_sum.at[0], {"dp": across}).wait_recv()
    tiles[2] = tiles[0] + tiles[1]
    begin(remote(tiles.at[2], tiles.at[3], send_sum.at[1], recv_sum.at[1], {"dp": partner}))
    take(near, mine, 1)
    take(near, across, 2)
    remote(tiles.at[2], tiles.at[3], send_sum.at[1], recv_sum.at[1], {"dp": partner}).wait_recv()
    for copy in outgoing:
        copy.wait_send()
    total_ref[...] = tiles[2] + tiles[3]


def reduce_step(gradient, squares):
    size, parts, members, rows, width = gradient.shape
    assert members == 4
    vmem = pl.BlockSpec(memory_space=pltpu.VMEM)
    dma = pltpu.SemaphoreType.DMA
    piece = (parts, rows, width)
    kind = jnp.bfloat16
    return pl.pallas_call(
        functools.partial(reduce_kernel, size, members),
        out_shape=(
            jax.ShapeDtypeStruct((parts, members, rows, width), kind),
            jax.ShapeDtypeStruct((16, 128), jnp.float32),
        ),
        in_specs=[vmem] * 2,
        out_specs=(vmem,) * 2,
        scratch_shapes=[
            pltpu.VMEM((2, size) + piece, kind),
            pltpu.VMEM((size,) + piece, kind),
            pltpu.VMEM((size,) + piece, kind),
            pltpu.VMEM((size,) + piece, kind),
            pltpu.VMEM((size,) + piece, kind),
            pltpu.VMEM((4, 16, 128), jnp.float32),
            pltpu.VMEM((size, 16, 128), jnp.float32),
            dma((2, size)), dma((2, size)), dma((size,)), dma((size,)), dma((size,)),
            dma((size,)), dma((size,)), dma((size,)), dma((3,)), dma((3,)), dma((2,)), dma((2,)),
        ],
        compiler_params=pltpu.CompilerParams(
            collective_id=1, has_side_effects=True, vmem_limit_bytes=48 * 1024 * 1024
        ),
    )(gradient, squares)


def fused_kernel(
    size, members, windows, length,
    signal_ref, weight_ref, first_ref, second_ref, shuffle_ref,
    rec_ref, mean_ref, direction_ref, back_ref,
    onehot, table, pre, act, back, partial, wide, full, first, last, before, after,
    grad, square, halves, passed, crossed, kept, incoming, own_total, tiles, tile_in, owned_ref, total_ref,
    send_halo, recv_halo, send_w, recv_w, send_f, recv_f,
    send_core, recv_core, send_x, recv_x, send_tm, recv_tm, send_tile, recv_tile,
    send_gather, recv_gather, send_sum, recv_sum,
):
    me, mine = lax.axis_index("tm"), lax.axis_index("dp")
    bits = bits_of(members)
    near, far = bits
    partner, across = flip(mine, near), flip(mine, far)
    corner = flip(partner, far)
    channels = signal_ref.shape[2]
    blocks = channels // WIDE
    parts = blocks // size
    quarter_rows = KERNEL * GW // members
    step = length + 2 * HALO
    rows = windows * step
    outgoing = []

    def begin(copy):
        copy.start()
        outgoing.append(copy)
        return copy

    for p in range(parts):
        for d in range(members):
            full[me, p, d] = weight_ref[
                d * quarter_rows : (d + 1) * quarter_rows, p * WIDE : (p + 1) * WIDE
            ].astype(full.dtype)
    first[...] = jnp.concatenate(
        [signal_ref[w, 0:16, :].astype(jnp.float32)[:HALO] for w in range(windows)], axis=0
    ).astype(first.dtype)
    last[...] = jnp.concatenate(
        [
            signal_ref[w, length - 16 : length, :].astype(jnp.float32)[16 - HALO :]
            for w in range(windows)
        ],
        axis=0,
    ).astype(last.dtype)

    greet(me, size, members, bits, mine)
    target = [lax.rem(me + j, size) for j in range(size)]
    source = [lax.rem(me - j + size, size) for j in range(size)]
    to_after = remote(
        last, before, send_halo.at[0], recv_halo.at[0], {"tm": jnp.minimum(me + 1, size - 1)}
    )
    to_before = remote(
        first, after, send_halo.at[1], recv_halo.at[1], {"tm": jnp.maximum(me - 1, 0)}
    )

    @pl.when(me < size - 1)
    def _():
        to_after.start()

    @pl.when(me > 0)
    def _():
        to_before.start()

    for j in range(1, size):
        begin(
            remote(
                full.at[me, :, mine], full.at[me, :, mine], send_w.at[j], recv_w.at[j],
                {"tm": target[j]},
            )
        )

    @pl.when(me == 0)
    def _():
        before[...] = jnp.zeros_like(before)

    @pl.when(me == size - 1)
    def _():
        after[...] = jnp.zeros_like(after)

    square[...] = jnp.zeros_like(square)

    def mark(index, carry):
        cols = pl.ds(pl.multiple_of(index * WIDE, WIDE), WIDE)
        row = lax.broadcasted_iota(jnp.int32, (channels, WIDE), 0)
        onehot[:, cols] = jnp.where(row == shuffle_ref[:, cols], 1.0, 0.0).astype(jnp.bfloat16)
        return carry

    lax.fori_loop(0, blocks, mark, 0)

    def weight_copy(origin, quarter, landed, level, j, where):
        return remote(
            full.at[origin, :, quarter], full.at[origin, :, landed], send_f.at[level, j],
            recv_f.at[level, j], {"dp": where},
        )

    for j in range(1, size):
        remote(
            full.at[me, :, mine], full.at[source[j], :, mine], send_w.at[j], recv_w.at[j],
            {"tm": source[j]},
        ).wait_recv()
        begin(weight_copy(source[j], mine, mine, 0, j, across))
        begin(weight_copy(source[j], mine, mine, 1, j, partner))

    @pl.when(me < size - 1)
    def _():
        to_after.wait_send()
        to_before.wait_recv()

    @pl.when(me > 0)
    def _():
        to_before.wait_send()
        to_after.wait_recv()

    place = lax.broadcasted_iota(jnp.int32, (rows, WIDE), 0)
    inner = lax.rem(place, step)
    low = jnp.where(me == 0, HALO, 0)
    high = jnp.where(me == size - 1, HALO + length, step)
    inside = jnp.logical_and(inner >= low, inner < high)
    block_mask = (
        lax.broadcasted_iota(jnp.int32, (WIDE, WIDE), 0) // GW
        == lax.broadcasted_iota(jnp.int32, (WIDE, WIDE), 1) // GW
    )

    def encode_from(origin):
        def encode(p, carry):
            index = origin * parts + p
            cols = pl.ds(pl.multiple_of(index * WIDE, WIDE), WIDE)
            weights = full[origin, p].astype(jnp.float32).reshape(KERNEL * GW, WIDE)
            for k in range(KERNEL):
                tiled = jnp.concatenate([weights[k * GW : (k + 1) * GW]] * (WIDE // GW), axis=0)
                table[index, k * WIDE : (k + 1) * WIDE, :] = jnp.where(
                    block_mask, tiled, 0.0
                ).astype(jnp.bfloat16)
            head = before[:, cols].astype(jnp.float32)
            tail = after[:, cols].astype(jnp.float32)
            pieces = []
            for w in range(windows):
                pieces += [
                    head[w * HALO : (w + 1) * HALO],
                    signal_ref[w, :, cols].astype(jnp.float32),
                    tail[w * HALO : (w + 1) * HALO],
                ]
            x = jnp.concatenate(pieces, axis=0)
            wide[:, cols] = x.astype(jnp.bfloat16)
            stack = jnp.concatenate(
                [shifted(x, 2 - k).astype(jnp.bfloat16) for k in range(KERNEL)], axis=1
            )
            value = jnp.dot(stack, table[index], preferred_element_type=jnp.float32)
            pre[:, cols] = local_part(value, windows, length)
            active = value / (1.0 + jnp.exp(-value))
            act[:, cols] = jnp.where(inside, active, 0.0).astype(jnp.bfloat16)
            return carry

        lax.fori_loop(0, parts, encode, 0)

    encode_from(me)
    for j in range(1, size):
        weight_copy(source[j], mine, across, 0, j, across).wait_recv()
        begin(weight_copy(source[j], across, across, 2, j, partner))
    for j in range(1, size):
        weight_copy(source[j], mine, partner, 1, j, partner).wait_recv()
        weight_copy(source[j], across, corner, 2, j, partner).wait_recv()
        encode_from(source[j])

    def decode(index, carry):
        cols = pl.ds(pl.multiple_of(index * WIDE, WIDE), WIDE)
        mixed = jnp.dot(act[...], onehot[:, cols], preferred_element_type=jnp.float32)
        decoded = jnp.zeros((rows, WIDE), jnp.float32)
        own_mixed = []
        for k in range(KERNEL):
            moved = shifted(mixed, k - 2)
            own_mixed.append(local_part(moved, windows, length).astype(jnp.bfloat16))
            decoded += lax.dot_general(
                moved.astype(jnp.bfloat16),
                table[index, k * WIDE : (k + 1) * WIDE, :],
                NT,
                preferred_element_type=jnp.float32,
            )
        error = jnp.where(inside, decoded - wide[:, cols].astype(jnp.float32), 0.0)
        own_decoded = local_part(decoded, windows, length).astype(jnp.bfloat16)
        for w in range(windows):
            rec_ref[w, :, cols] = own_decoded[w * length : (w + 1) * length]
        own_error = local_part(error, windows, length)
        square[...] += (own_error * own_error).reshape(-1, 8, WIDE).sum(axis=0)
        stack = jnp.concatenate(
            [shifted(error, 2 - k).astype(jnp.bfloat16) for k in range(KERNEL)], axis=1
        )
        value = jnp.dot(stack, table[index], preferred_element_type=jnp.float32)
        back[:, cols] = local_part(value, windows, length).astype(jnp.bfloat16)
        product = lax.dot_general(
            own_error.astype(jnp.bfloat16),
            jnp.concatenate(own_mixed, axis=1),
            TN,
            preferred_element_type=jnp.float32,
        )
        for k in range(KERNEL):
            partial[index, k * GW : (k + 1) * GW, :] = diagonal(
                product[:, k * WIDE : (k + 1) * WIDE]
            )
        return carry

    lax.fori_loop(0, blocks, decode, 0)

    def finish_for(owner):
        def finish(p, carry):
            index = owner * parts + p
            start = pl.multiple_of(index * WIDE, WIDE)
            cols = pl.ds(start, WIDE)
            restored = lax.dot_general(
                back[...], onehot[pl.ds(start, WIDE), :], NT, preferred_element_type=jnp.float32
            )
            value = pre[:, cols]
            sigma = 1.0 / (1.0 + jnp.exp(-value))
            own = (restored * (sigma * (1.0 + value * (1.0 - sigma)))).astype(jnp.bfloat16)
            for w in range(windows):
                back_ref[w, :, cols] = own[w * length : (w + 1) * length]
            spread = spread_part(own.astype(jnp.float32), windows, length)
            stack = jnp.concatenate(
                [shifted(spread, k - 2).astype(jnp.bfloat16) for k in range(KERNEL)], axis=1
            )
            product = lax.dot_general(wide[:, cols], stack, TN, preferred_element_type=jnp.float32)
            total = partial[index] + jnp.concatenate(
                [diagonal(product[:, k * WIDE : (k + 1) * WIDE]) for k in range(KERNEL)], axis=0
            )
            grad[owner, p] = total.reshape(members, quarter_rows, WIDE).astype(grad.dtype)
            return carry

        lax.fori_loop(0, parts, finish, 0)

    core, x = {}, {}

    def send_core_chunk(j):
        for slot, quarter in ((1, corner), (0, partner)):
            core[slot, j] = begin(
                remote(
                    grad.at[target[j], :, quarter], halves.at[slot, j], send_core.at[slot, j],
                    recv_core.at[slot, j], {"dp": partner},
                )
            )

    def send_x_chunk(j):
        core[1, j].wait_recv()
        passed[j] = (
            grad[target[j], :, across].astype(jnp.float32) + halves[1, j].astype(jnp.float32)
        ).astype(passed.dtype)
        x[j] = begin(
            remote(passed.at[j], crossed.at[j], send_x.at[j], recv_x.at[j], {"dp": across})
        )

    def send_tm_chunk(j):
        core[0, j].wait_recv()
        x[j].wait_recv()
        value = (
            grad[target[j], :, mine].astype(jnp.float32)
            + halves[0, j].astype(jnp.float32)
            + crossed[j].astype(jnp.float32)
        )
        if j == 0:
            own_total[...] = value
        else:
            kept[j] = value.astype(kept.dtype)
            begin(
                remote(
                    kept.at[j], incoming.at[j], send_tm.at[j], recv_tm.at[j], {"tm": target[j]}
                )
            )

    order = list(range(1, size)) + [0]
    for n in range(size + 2):
        if n < size:
            finish_for(target[order[n]])
            send_core_chunk(order[n])
        if 1 <= n <= size:
            send_x_chunk(order[n - 1])
        if n >= 2:
            send_tm_chunk(order[n - 2])

    total = own_total[...]
    for j in range(1, size):
        remote(
            kept.at[j], incoming.at[j], send_tm.at[j], recv_tm.at[j], {"tm": source[j]}
        ).wait_recv()
        total = total + incoming[j].astype(jnp.float32)
    rounded = total.astype(owned_ref.dtype)
    owned_ref[:, mine] = rounded

    def share(bit, quarter, number):
        return begin(
            remote(
                owned_ref.at[:, quarter], owned_ref.at[:, quarter], send_gather.at[number],
                recv_gather.at[number], {"dp": flip(mine, bit)},
            )
        )

    def take(bit, quarter, number):
        remote(
            owned_ref.at[:, flip(quarter, bit)], owned_ref.at[:, flip(quarter, bit)],
            send_gather.at[number], recv_gather.at[number], {"dp": flip(mine, bit)},
        ).wait_recv()

    back = rounded.astype(jnp.float32)
    powers = (back * back).reshape(-1, 8, back.shape[-1]).sum(axis=0)
    total_ref[...] = jnp.zeros_like(total_ref)
    width = powers.shape[-1]
    if width % 128 == 0:
        folded = powers[:, :128]
        for n in range(1, width // 128):
            folded = folded + powers[:, n * 128 : (n + 1) * 128]
        total_ref[8:16, :] = folded
    else:
        total_ref[8:16, :width] = powers
    total_ref[0:8, :] = square[:, :128] + square[:, 128:]
    tile_in[me] = total_ref[...]
    for j in range(1, size):
        begin(
            remote(
                total_ref, tile_in.at[me], send_tile.at[j], recv_tile.at[j], {"tm": target[j]}
            )
        )
    share(far, mine, 0)
    share(near, mine, 1)
    for j in range(1, size):
        remote(
            total_ref, tile_in.at[source[j]], send_tile.at[j], recv_tile.at[j], {"tm": source[j]}
        ).wait_recv()
    tiles[0] = tile_in[...].sum(axis=0)
    begin(remote(tiles.at[0], tiles.at[1], send_sum.at[0], recv_sum.at[0], {"dp": across}))
    take(far, mine, 0)
    share(near, across, 2)
    remote(tiles.at[0], tiles.at[1], send_sum.at[0], recv_sum.at[0], {"dp": across}).wait_recv()
    tiles[2] = tiles[0] + tiles[1]
    begin(remote(tiles.at[2], tiles.at[3], send_sum.at[1], recv_sum.at[1], {"dp": partner}))
    take(near, mine, 1)
    take(near, across, 2)
    remote(tiles.at[2], tiles.at[3], send_sum.at[1], recv_sum.at[1], {"dp": partner}).wait_recv()
    for copy in outgoing:
        copy.wait_send()
    sums = tiles[2] + tiles[3]
    count = windows * members * length * size * channels
    mean_ref[...] = jnp.sum(sums[:8], axis=(0, 1), keepdims=True) / count
    square_total = jnp.sum(sums[8:], axis=(0, 1), keepdims=True)
    for p in range(parts):
        lanes = slice(p * WIDE, (p + 1) * WIDE)
        for d in range(members):
            taken = slice(d * quarter_rows, (d + 1) * quarter_rows)
            direction_ref[taken, lanes] = adam_direction(
                owned_ref[p, d].astype(jnp.float32), square_total, KW * CH,
                weight_ref[taken, lanes], first_ref[taken, lanes], second_ref[taken, lanes],
            )


def fused_step(signal, weight, first_moment, second_moment, shuffle):
    size, members = lax.axis_size("tm"), lax.axis_size("dp")
    assert members == 4
    windows, length, channels = signal.shape
    depth, cols = weight.shape
    parts, blocks, quarter = cols // WIDE, channels // WIDE, depth // members
    own, rows = windows * length, windows * (length + 2 * HALO)
    vmem = pl.BlockSpec(memory_space=pltpu.VMEM)
    dma = pltpu.SemaphoreType.DMA
    kind = jnp.bfloat16
    piece = (parts, quarter, WIDE)
    everything = (size, parts, members, quarter, WIDE)
    edge = pltpu.VMEM((windows * HALO, channels), kind)
    return pl.pallas_call(
        functools.partial(fused_kernel, size, members, windows, length),
        out_shape=(
            jax.ShapeDtypeStruct(signal.shape, kind),
            jax.ShapeDtypeStruct((1, 1), jnp.float32),
            jax.ShapeDtypeStruct(weight.shape, jnp.float32),
            jax.ShapeDtypeStruct(signal.shape, kind),
        ),
        in_specs=[vmem] * 5,
        out_specs=(vmem,) * 4,
        scratch_shapes=[
            pltpu.VMEM((channels, channels), kind),
            pltpu.VMEM((blocks, KERNEL * WIDE, WIDE), kind),
            pltpu.VMEM((own, channels), jnp.float32),
            pltpu.VMEM((rows, channels), kind),
            pltpu.VMEM((own, channels), kind),
            pltpu.VMEM((blocks, depth, WIDE), jnp.float32),
            pltpu.VMEM((rows, channels), kind),
            pltpu.VMEM(everything, kind),
            edge, edge, edge, edge,
            pltpu.VMEM(everything, kind),
            pltpu.VMEM((8, WIDE), jnp.float32),
            pltpu.VMEM((2, size) + piece, kind),
            pltpu.VMEM((size,) + piece, kind),
            pltpu.VMEM((size,) + piece, kind),
            pltpu.VMEM((size,) + piece, kind),
            pltpu.VMEM((size,) + piece, kind),
            pltpu.VMEM(piece, jnp.float32),
            pltpu.VMEM((4, 16, 128), jnp.float32),
            pltpu.VMEM((size, 16, 128), jnp.float32),
            pltpu.VMEM((parts, members, quarter, WIDE), kind),
            pltpu.VMEM((16, 128), jnp.float32),
            dma((2,)), dma((2,)), dma((size,)), dma((size,)), dma((3, size)), dma((3, size)),
            dma((2, size)), dma((2, size)), dma((size,)), dma((size,)), dma((size,)),
            dma((size,)), dma((size,)), dma((size,)), dma((3,)), dma((3,)), dma((2,)), dma((2,)),
        ],
        compiler_params=pltpu.CompilerParams(
            collective_id=2, has_side_effects=True, vmem_limit_bytes=56 * 1024 * 1024
        ),
    )(signal, weight, first_moment, second_moment, shuffle.reshape(1, channels))


def adam_direction(grad_part, square_total, entries, weight_part, first_part, second_part):
    rms_value = jnp.sqrt(square_total / entries + rms_eps)
    factor = jnp.minimum(1.0, 1.0 / rms_value)
    clipped = grad_part * factor
    first_new = beta_one * first_part + (1.0 - beta_one) * clipped
    second_new = beta_two * second_part + (1.0 - beta_two) * clipped * clipped
    first_hat = first_new / (1.0 - beta_one**step_count)
    second_hat = second_new / (1.0 - beta_two**step_count)
    return first_hat / (jnp.sqrt(second_hat) + adam_eps) + decay_rate * weight_part


def on_device(signal, weight, first_moment, second_moment, shuffle):
    windows, length, channels = signal.shape
    size, members = lax.axis_size("tm"), lax.axis_size("dp")
    depth, cols = weight.shape
    width = WIDE if cols % WIDE == 0 else cols
    parts, blocks = cols // width, channels // WIDE
    rows = depth // members
    if cols % WIDE == 0:
        decoded, mean_error, direction, back_pre = fused_step(
            signal, weight, first_moment, second_moment, shuffle
        )
        return (decoded, mean_error.reshape(1), direction, back_pre)
    shard = weight.astype(jnp.bfloat16).reshape(members, rows, parts, width).transpose(2, 0, 1, 3)
    first = signal[:, :HALO].reshape(windows * HALO, channels)
    last = signal[:, length - HALO :].reshape(windows * HALO, channels)
    full, before, after = gather_step(shard, first, last)
    full = (
        full.reshape(blocks, WIDE // width, depth, width)
        .transpose(0, 2, 1, 3)
        .reshape(blocks, depth, WIDE)
    )
    before = before.reshape(windows, HALO, channels)
    after = after.reshape(windows, HALO, channels)
    decoded, back_pre, gradient, squares = local_step(signal, full, shuffle, before, after)
    gradient = (
        gradient.reshape(blocks, depth, WIDE // width, width)
        .transpose(0, 2, 1, 3)
        .reshape(size, parts, members, rows, width)
    )
    owned, totals = reduce_step(gradient, squares)
    element_count = windows * members * length * size * channels
    mean_error = (jnp.sum(totals[:8]) / element_count).reshape(1)
    owned = owned.transpose(1, 2, 0, 3).reshape(depth, cols).astype(jnp.float32)
    square_total = jnp.sum(totals[8:])
    direction = adam_direction(owned, square_total, KW * CH, weight, first_moment, second_moment)
    return (decoded, mean_error, direction, back_pre)


def solution(mesh):
    return jax.shard_map(
        on_device,
        mesh=mesh,
        in_specs=(
            P(("parts", "dp"), "tm", None),
            P("parts", "tm"),
            P("parts", "tm"),
            P("parts", "tm"),
            P(),
        ),
        out_specs=(
            P(("parts", "dp"), "tm", None),
            P("parts"),
            P("parts", "tm"),
            P(("parts", "dp"), "tm", None),
        ),
        check_vma=False,
    )
```

```python
import functools

import jax
import jax.numpy as jnp
from jax import lax
from jax.experimental import pallas as pl
from jax.experimental.pallas import tpu as pltpu
from jax.sharding import PartitionSpec as P

GW = 64
KERNEL = 5
CH = 2048
KW = 320
WIDE = 256
HALO = 8

beta_one = 0.9
beta_two = 0.999
adam_eps = 1e-08
decay_rate = 0.1
rms_eps = 1e-06
step_count = 100

MESH = pl.DeviceIdType.MESH
TN = (((0,), (0,)), ((), ()))
NT = (((1,), (1,)), ((), ()))


def shifted(value, amount):
    rows = value.shape[0]
    return value if amount % rows == 0 else pltpu.roll(value, amount % rows, 0)


def local_part(value, windows, length):
    step = length + 2 * HALO
    return jnp.concatenate(
        [value[w * step + HALO : w * step + HALO + length] for w in range(windows)], axis=0
    )


def spread_part(value, windows, length):
    blank = jnp.zeros((HALO, value.shape[1]), value.dtype)
    pieces = []
    for w in range(windows):
        pieces += [blank, value[w * length : (w + 1) * length], blank]
    return jnp.concatenate(pieces, axis=0)


def diagonal(value):
    lane = lax.broadcasted_iota(jnp.int32, (GW, WIDE), 1) // GW
    picked = value[:GW]
    for j in range(1, WIDE // GW):
        picked = jnp.where(lane == j, value[j * GW : (j + 1) * GW], picked)
    return picked


def compute_kernel(
    windows, length, sig_ref, w_ref, shuffle_ref, rec_ref, back_ref, grad_ref, square_ref,
    onehot, table, pre, act, back, partial,
):
    channels = sig_ref.shape[1]
    blocks = channels // WIDE
    rows = sig_ref.shape[0]
    step = length + 2 * HALO
    me, peers = lax.axis_index("tm"), lax.axis_size("tm")
    place = lax.broadcasted_iota(jnp.int32, (rows, WIDE), 0)
    inner = lax.rem(place, step)
    low = jnp.where(me == 0, HALO, 0)
    high = jnp.where(me == peers - 1, HALO + length, step)
    inside = jnp.logical_and(inner >= low, inner < high)
    block_mask = (
        lax.broadcasted_iota(jnp.int32, (WIDE, WIDE), 0) // GW
        == lax.broadcasted_iota(jnp.int32, (WIDE, WIDE), 1) // GW
    )
    square_ref[...] = jnp.zeros_like(square_ref)

    def encode(index, carry):
        cols = pl.ds(pl.multiple_of(index * WIDE, WIDE), WIDE)
        for k in range(KERNEL):
            taps = w_ref[index, k * GW : (k + 1) * GW, :].astype(jnp.float32)
            tiled = jnp.concatenate([taps] * (WIDE // GW), axis=0)
            table[index, k * WIDE : (k + 1) * WIDE, :] = jnp.where(block_mask, tiled, 0.0).astype(
                jnp.bfloat16
            )
        x = sig_ref[:, cols].astype(jnp.float32)
        stack = jnp.concatenate(
            [shifted(x, 2 - k).astype(jnp.bfloat16) for k in range(KERNEL)], axis=1
        )
        value = jnp.dot(stack, table[index], preferred_element_type=jnp.float32)
        pre[:, cols] = local_part(value, windows, length)
        active = value / (1.0 + jnp.exp(-value))
        act[:, cols] = jnp.where(inside, active, 0.0).astype(jnp.bfloat16)
        return carry

    lax.fori_loop(0, blocks, encode, 0)

    def decode(index, carry):
        cols = pl.ds(pl.multiple_of(index * WIDE, WIDE), WIDE)
        source = lax.broadcasted_iota(jnp.int32, (channels, WIDE), 0)
        onehot[:, cols] = jnp.where(source == shuffle_ref[:, cols], 1.0, 0.0).astype(jnp.bfloat16)
        mixed = jnp.dot(act[...], onehot[:, cols], preferred_element_type=jnp.float32)
        decoded = jnp.zeros((rows, WIDE), jnp.float32)
        own_mixed = []
        for k in range(KERNEL):
            moved = shifted(mixed, k - 2)
            own_mixed.append(local_part(moved, windows, length).astype(jnp.bfloat16))
            decoded += lax.dot_general(
                moved.astype(jnp.bfloat16),
                table[index, k * WIDE : (k + 1) * WIDE, :],
                NT,
                preferred_element_type=jnp.float32,
            )
        error = jnp.where(inside, decoded - sig_ref[:, cols].astype(jnp.float32), 0.0)
        own_decoded = local_part(decoded, windows, length).astype(jnp.bfloat16)
        for w in range(windows):
            rec_ref[w, :, cols] = own_decoded[w * length : (w + 1) * length]
        own_error = local_part(error, windows, length)
        square_ref[...] += (own_error * own_error).reshape(-1, 8, WIDE).sum(axis=0)
        stack = jnp.concatenate(
            [shifted(error, 2 - k).astype(jnp.bfloat16) for k in range(KERNEL)], axis=1
        )
        value = jnp.dot(stack, table[index], preferred_element_type=jnp.float32)
        back[:, cols] = local_part(value, windows, length).astype(jnp.bfloat16)
        product = lax.dot_general(
            own_error.astype(jnp.bfloat16),
            jnp.concatenate(own_mixed, axis=1),
            TN,
            preferred_element_type=jnp.float32,
        )
        for k in range(KERNEL):
            partial[k * GW : (k + 1) * GW, cols] = diagonal(product[:, k * WIDE : (k + 1) * WIDE])
        return carry

    lax.fori_loop(0, blocks, decode, 0)

    def finish(index, carry):
        start = pl.multiple_of(index * WIDE, WIDE)
        cols = pl.ds(start, WIDE)
        restored = lax.dot_general(
            back[...], onehot[pl.ds(start, WIDE), :], NT, preferred_element_type=jnp.float32
        )
        value = pre[:, cols]
        sigma = 1.0 / (1.0 + jnp.exp(-value))
        own = (restored * (sigma * (1.0 + value * (1.0 - sigma)))).astype(jnp.bfloat16)
        for w in range(windows):
            back_ref[w, :, cols] = own[w * length : (w + 1) * length]
        wide = spread_part(own.astype(jnp.float32), windows, length)
        stack = jnp.concatenate(
            [shifted(wide, k - 2).astype(jnp.bfloat16) for k in range(KERNEL)], axis=1
        )
        product = lax.dot_general(
            sig_ref[:, cols], stack, TN, preferred_element_type=jnp.float32
        )
        for k in range(KERNEL):
            taken = slice(k * GW, (k + 1) * GW)
            total = partial[taken, cols] + diagonal(product[:, k * WIDE : (k + 1) * WIDE])
            grad_ref[index, taken, :] = total.astype(grad_ref.dtype)
        return carry

    lax.fori_loop(0, blocks, finish, 0)


def local_step(signal, weight, shuffle, before, after):
    windows, length, channels = signal.shape
    wide = jnp.concatenate([before, signal, after], axis=1)
    rows = windows * (length + 2 * HALO)
    vmem = pl.BlockSpec(memory_space=pltpu.VMEM)
    own = windows * length
    return pl.pallas_call(
        functools.partial(compute_kernel, windows, length),
        out_shape=(
            jax.ShapeDtypeStruct(signal.shape, jnp.bfloat16),
            jax.ShapeDtypeStruct(signal.shape, jnp.bfloat16),
            jax.ShapeDtypeStruct((channels // WIDE, KERNEL * GW, WIDE), jnp.bfloat16),
            jax.ShapeDtypeStruct((8, WIDE), jnp.float32),
        ),
        in_specs=[vmem] * 3,
        out_specs=(vmem,) * 4,
        scratch_shapes=[
            pltpu.VMEM((channels, channels), jnp.bfloat16),
            pltpu.VMEM((channels // WIDE, KERNEL * WIDE, WIDE), jnp.bfloat16),
            pltpu.VMEM((own, channels), jnp.float32),
            pltpu.VMEM((rows, channels), jnp.bfloat16),
            pltpu.VMEM((own, channels), jnp.bfloat16),
            pltpu.VMEM((KERNEL * GW, channels), jnp.float32),
        ],
        compiler_params=pltpu.CompilerParams(vmem_limit_bytes=48 * 1024 * 1024),
    )(wide.reshape(rows, channels), weight, shuffle.reshape(1, channels))


def flip(index, bit):
    return index + bit - 2 * bit * ((index // bit) % 2)


def bits_of(count):
    return [1 << b for b in range(count.bit_length() - 1)]


def greet(peers, size, members, bits, mine):
    barrier = pltpu.get_barrier_semaphore()
    for j in range(1, size):
        pl.semaphore_signal(
            barrier, inc=1, device_id={"tm": lax.rem(peers + j, size)}, device_id_type=MESH
        )
    for bit in bits:
        pl.semaphore_signal(
            barrier, inc=1, device_id={"dp": flip(mine, bit)}, device_id_type=MESH
        )
    pl.semaphore_wait(barrier, size - 1 + len(bits))


def remote(src, dst, send, recv, target):
    return pltpu.make_async_remote_copy(
        src_ref=src, dst_ref=dst, send_sem=send, recv_sem=recv, device_id=target,
        device_id_type=MESH,
    )


def gather_kernel(
    size, members, shard_ref, first_ref, last_ref, full_ref, before_ref, after_ref,
    send_tm, recv_tm, send_dp, recv_dp, send_halo, recv_halo, local_sem,
):
    me, mine = lax.axis_index("tm"), lax.axis_index("dp")
    bits = bits_of(members)
    greet(me, size, members, bits, mine)

    to_after = remote(
        last_ref, before_ref, send_halo.at[0], recv_halo.at[0], {"tm": jnp.minimum(me + 1, size - 1)}
    )
    to_before = remote(
        first_ref, after_ref, send_halo.at[1], recv_halo.at[1], {"tm": jnp.maximum(me - 1, 0)}
    )

    @pl.when(me < size - 1)
    def _():
        to_after.start()

    @pl.when(me > 0)
    def _():
        to_before.start()

    outgoing = []
    for j in range(1, size):
        copy = remote(
            shard_ref.at[:, mine],
            full_ref.at[me, :, mine],
            send_tm.at[j],
            recv_tm.at[j],
            {"tm": lax.rem(me + j, size)},
        )
        copy.start()
        outgoing.append(copy)
    keep = pltpu.make_async_copy(shard_ref, full_ref.at[me], local_sem)
    keep.start()

    @pl.when(me == 0)
    def _():
        before_ref[...] = jnp.zeros_like(before_ref)

    @pl.when(me == size - 1)
    def _():
        after_ref[...] = jnp.zeros_like(after_ref)

    owned = [mine]
    number = 0
    for level, bit in enumerate(reversed(bits)):
        for j in range(1, size):
            source = lax.rem(me - j + size, size)
            if level == 0:
                remote(
                    shard_ref.at[:, mine],
                    full_ref.at[source, :, mine],
                    send_tm.at[j],
                    recv_tm.at[j],
                    {"tm": source},
                ).wait_recv()
            else:
                for copy in pending[j]:
                    copy.wait_recv()
            for place, quarter in enumerate(owned):
                copy = remote(
                    full_ref.at[source, :, quarter],
                    full_ref.at[source, :, quarter],
                    send_dp.at[number + place, j],
                    recv_dp.at[number + place, j],
                    {"dp": flip(mine, bit)},
                )
                copy.start()
                outgoing.append(copy)
        pending = {
            j: [
                remote(
                    full_ref.at[lax.rem(me - j + size, size), :, quarter],
                    full_ref.at[lax.rem(me - j + size, size), :, flip(quarter, bit)],
                    send_dp.at[number + place, j],
                    recv_dp.at[number + place, j],
                    {"dp": flip(mine, bit)},
                )
                for place, quarter in enumerate(owned)
            ]
            for j in range(1, size)
        }
        number += len(owned)
        owned = owned + [flip(quarter, bit) for quarter in owned]
    for j in range(1, size):
        for copy in pending[j]:
            copy.wait_recv()
    for copy in outgoing:
        copy.wait_send()
    keep.wait()

    @pl.when(me < size - 1)
    def _():
        to_after.wait_send()
        to_before.wait_recv()

    @pl.when(me > 0)
    def _():
        to_before.wait_send()
        to_after.wait_recv()


def gather_step(shard, first, last):
    size, members = lax.axis_size("tm"), lax.axis_size("dp")
    vmem = pl.BlockSpec(memory_space=pltpu.VMEM)
    dma = pltpu.SemaphoreType.DMA
    return pl.pallas_call(
        functools.partial(gather_kernel, size, members),
        out_shape=(
            jax.ShapeDtypeStruct((size,) + shard.shape, shard.dtype),
            jax.ShapeDtypeStruct(first.shape, first.dtype),
            jax.ShapeDtypeStruct(last.shape, last.dtype),
        ),
        in_specs=[vmem] * 3,
        out_specs=(vmem,) * 3,
        scratch_shapes=[
            dma((size,)), dma((size,)), dma((members, size)), dma((members, size)),
            dma((2,)), dma((2,)), dma,
        ],
        compiler_params=pltpu.CompilerParams(
            collective_id=0, has_side_effects=True, vmem_limit_bytes=32 * 1024 * 1024
        ),
    )(shard, first, last)


def reduce_kernel(
    size, members, grad_ref, square_ref, owned_ref, total_ref,
    halves, passed, crossed, kept, incoming, tiles, tile_in,
    send_core, recv_core, send_x, recv_x, send_tm, recv_tm, send_tile, recv_tile,
    send_gather, recv_gather, send_sum, recv_sum,
):
    me, mine = lax.axis_index("tm"), lax.axis_index("dp")
    bits = bits_of(members)
    near, far = bits
    partner, across = flip(mine, near), flip(mine, far)
    corner = flip(partner, far)
    greet(me, size, members, bits, mine)
    outgoing = []

    def begin(copy):
        copy.start()
        outgoing.append(copy)
        return copy

    order = list(range(1, size)) + [0]
    target = [lax.rem(me + j, size) for j in range(size)]
    core = {}
    for slot, quarter in ((1, corner), (0, partner)):
        for j in order:
            core[slot, j] = begin(
                remote(
                    grad_ref.at[target[j], :, quarter],
                    halves.at[slot, target[j]],
                    send_core.at[slot, j],
                    recv_core.at[slot, j],
                    {"dp": partner},
                )
            )
    x = {}
    for j in order:
        core[1, j].wait_recv()
        passed[target[j]] = (
            grad_ref[target[j], :, across].astype(jnp.float32)
            + halves[1, target[j]].astype(jnp.float32)
        ).astype(passed.dtype)
        x[j] = begin(
            remote(
                passed.at[target[j]], crossed.at[target[j]], send_x.at[j], recv_x.at[j],
                {"dp": across},
            )
        )
    for j in order:
        core[0, j].wait_recv()
        x[j].wait_recv()
        value = (
            grad_ref[target[j], :, mine].astype(jnp.float32)
            + halves[0, target[j]].astype(jnp.float32)
            + crossed[target[j]].astype(jnp.float32)
        )
        if j == 0:
            total = value
        else:
            kept[j] = value.astype(kept.dtype)
            begin(
                remote(
                    kept.at[j], incoming.at[j], send_tm.at[j], recv_tm.at[j], {"tm": target[j]}
                )
            )
    for j in range(1, size):
        source = lax.rem(me - j + size, size)
        remote(
            kept.at[j], incoming.at[j], send_tm.at[j], recv_tm.at[j], {"tm": source}
        ).wait_recv()
        total = total + incoming[j].astype(jnp.float32)
    rounded = total.astype(owned_ref.dtype)
    owned_ref[:, mine] = rounded

    def share(bit, quarter, number):
        return begin(
            remote(
                owned_ref.at[:, quarter], owned_ref.at[:, quarter], send_gather.at[number],
                recv_gather.at[number], {"dp": flip(mine, bit)},
            )
        )

    def take(bit, quarter, number):
        remote(
            owned_ref.at[:, flip(quarter, bit)], owned_ref.at[:, flip(quarter, bit)],
            send_gather.at[number], recv_gather.at[number], {"dp": flip(mine, bit)},
        ).wait_recv()

    back = rounded.astype(jnp.float32)
    powers = (back * back).reshape(-1, 8, back.shape[-1]).sum(axis=0)
    total_ref[...] = jnp.zeros_like(total_ref)
    width = powers.shape[-1]
    if width % 128 == 0:
        folded = powers[:, :128]
        for n in range(1, width // 128):
            folded = folded + powers[:, n * 128 : (n + 1) * 128]
        total_ref[8:16, :] = folded
    else:
        total_ref[8:16, :width] = powers
    total_ref[0:8, :] = square_ref[:, :128] + square_ref[:, 128:]
    tile_in[me] = total_ref[...]
    for j in range(1, size):
        begin(
            remote(
                total_ref, tile_in.at[me], send_tile.at[j], recv_tile.at[j], {"tm": target[j]}
            )
        )
    share(far, mine, 0)
    share(near, mine, 1)
    for j in range(1, size):
        source = lax.rem(me - j + size, size)
        remote(
            total_ref, tile_in.at[source], send_tile.at[j], recv_tile.at[j], {"tm": source}
        ).wait_recv()
    tiles[0] = tile_in[...].sum(axis=0)
    begin(remote(tiles.at[0], tiles.at[1], send_sum.at[0], recv_sum.at[0], {"dp": across}))
    take(far, mine, 0)
    share(near, across, 2)
    remote(tiles.at[0], tiles.at[1], send_sum.at[0], recv_sum.at[0], {"dp": across}).wait_recv()
    tiles[2] = tiles[0] + tiles[1]
    begin(remote(tiles.at[2], tiles.at[3], send_sum.at[1], recv_sum.at[1], {"dp": partner}))
    take(near, mine, 1)
    take(near, across, 2)
    remote(tiles.at[2], tiles.at[3], send_sum.at[1], recv_sum.at[1], {"dp": partner}).wait_recv()
    for copy in outgoing:
        copy.wait_send()
    total_ref[...] = tiles[2] + tiles[3]


def reduce_step(gradient, squares):
    size, parts, members, rows, width = gradient.shape
    assert members == 4
    vmem = pl.BlockSpec(memory_space=pltpu.VMEM)
    dma = pltpu.SemaphoreType.DMA
    piece = (parts, rows, width)
    kind = jnp.bfloat16
    return pl.pallas_call(
        functools.partial(reduce_kernel, size, members),
        out_shape=(
            jax.ShapeDtypeStruct((parts, members, rows, width), kind),
            jax.ShapeDtypeStruct((16, 128), jnp.float32),
        ),
        in_specs=[vmem] * 2,
        out_specs=(vmem,) * 2,
        scratch_shapes=[
            pltpu.VMEM((2, size) + piece, kind),
            pltpu.VMEM((size,) + piece, kind),
            pltpu.VMEM((size,) + piece, kind),
            pltpu.VMEM((size,) + piece, kind),
            pltpu.VMEM((size,) + piece, kind),
            pltpu.VMEM((4, 16, 128), jnp.float32),
            pltpu.VMEM((size, 16, 128), jnp.float32),
            dma((2, size)), dma((2, size)), dma((size,)), dma((size,)), dma((size,)),
            dma((size,)), dma((size,)), dma((size,)), dma((3,)), dma((3,)), dma((2,)), dma((2,)),
        ],
        compiler_params=pltpu.CompilerParams(
            collective_id=1, has_side_effects=True, vmem_limit_bytes=48 * 1024 * 1024
        ),
    )(gradient, squares)


def in_pairs(count, body):
    if count % 2:
        lax.fori_loop(0, count, body, 0)
        return

    def both(index, carry):
        return body(2 * index + 1, body(2 * index, carry))

    lax.fori_loop(0, count // 2, both, 0)


def fused_kernel(
    size, members, windows, length,
    signal_ref, weight_ref, first_ref, second_ref, shuffle_ref,
    rec_ref, mean_ref, direction_ref, back_ref,
    onehot, table, pre, act, back, partial, wide, full, first, last, before, after,
    grad, square, halves, passed, crossed, kept, incoming, own_total, tiles, tile_in, owned_ref, total_ref,
    send_halo, recv_halo, send_w, recv_w, send_f, recv_f,
    send_core, recv_core, send_x, recv_x, send_tm, recv_tm, send_tile, recv_tile,
    send_gather, recv_gather, send_sum, recv_sum,
):
    me, mine = lax.axis_index("tm"), lax.axis_index("dp")
    bits = bits_of(members)
    near, far = bits
    partner, across = flip(mine, near), flip(mine, far)
    corner = flip(partner, far)
    channels = signal_ref.shape[2]
    blocks = channels // WIDE
    parts = blocks // size
    quarter_rows = KERNEL * GW // members
    step = length + 2 * HALO
    rows = windows * step
    outgoing = []

    def begin(copy):
        copy.start()
        outgoing.append(copy)
        return copy

    for p in range(parts):
        for d in range(members):
            full[me, p, d] = weight_ref[
                d * quarter_rows : (d + 1) * quarter_rows, p * WIDE : (p + 1) * WIDE
            ].astype(full.dtype)
    first[...] = jnp.concatenate(
        [signal_ref[w, 0:16, :].astype(jnp.float32)[:HALO] for w in range(windows)], axis=0
    ).astype(first.dtype)
    last[...] = jnp.concatenate(
        [
            signal_ref[w, length - 16 : length, :].astype(jnp.float32)[16 - HALO :]
            for w in range(windows)
        ],
        axis=0,
    ).astype(last.dtype)

    greet(me, size, members, bits, mine)
    target = [lax.rem(me + j, size) for j in range(size)]
    source = [lax.rem(me - j + size, size) for j in range(size)]
    to_after = remote(
        last, before, send_halo.at[0], recv_halo.at[0], {"tm": jnp.minimum(me + 1, size - 1)}
    )
    to_before = remote(
        first, after, send_halo.at[1], recv_halo.at[1], {"tm": jnp.maximum(me - 1, 0)}
    )

    @pl.when(me < size - 1)
    def _():
        to_after.start()

    @pl.when(me > 0)
    def _():
        to_before.start()

    for j in range(1, size):
        begin(
            remote(
                full.at[me, :, mine], full.at[me, :, mine], send_w.at[j], recv_w.at[j],
                {"tm": target[j]},
            )
        )

    @pl.when(me == 0)
    def _():
        before[...] = jnp.zeros_like(before)

    @pl.when(me == size - 1)
    def _():
        after[...] = jnp.zeros_like(after)

    square[...] = jnp.zeros_like(square)

    def mark(index, carry):
        cols = pl.ds(pl.multiple_of(index * WIDE, WIDE), WIDE)
        row = lax.broadcasted_iota(jnp.int32, (channels, WIDE), 0)
        onehot[:, cols] = jnp.where(row == shuffle_ref[:, cols], 1.0, 0.0).astype(jnp.bfloat16)
        return carry

    lax.fori_loop(0, blocks, mark, 0)

    def weight_copy(origin, quarter, landed, level, j, where):
        return remote(
            full.at[origin, :, quarter], full.at[origin, :, landed], send_f.at[level, j],
            recv_f.at[level, j], {"dp": where},
        )

    for j in range(1, size):
        remote(
            full.at[me, :, mine], full.at[source[j], :, mine], send_w.at[j], recv_w.at[j],
            {"tm": source[j]},
        ).wait_recv()
        begin(weight_copy(source[j], mine, mine, 0, j, across))
        begin(weight_copy(source[j], mine, mine, 1, j, partner))

    @pl.when(me < size - 1)
    def _():
        to_after.wait_send()
        to_before.wait_recv()

    @pl.when(me > 0)
    def _():
        to_before.wait_send()
        to_after.wait_recv()

    place = lax.broadcasted_iota(jnp.int32, (rows, WIDE), 0)
    inner = lax.rem(place, step)
    low = jnp.where(me == 0, HALO, 0)
    high = jnp.where(me == size - 1, HALO + length, step)
    inside = jnp.logical_and(inner >= low, inner < high)
    block_mask = (
        lax.broadcasted_iota(jnp.int32, (WIDE, WIDE), 0) // GW
        == lax.broadcasted_iota(jnp.int32, (WIDE, WIDE), 1) // GW
    )

    def encode_from(origin):
        def encode(p, carry):
            index = origin * parts + p
            cols = pl.ds(pl.multiple_of(index * WIDE, WIDE), WIDE)
            weights = full[origin, p].astype(jnp.float32).reshape(KERNEL * GW, WIDE)
            for k in range(KERNEL):
                tiled = jnp.concatenate([weights[k * GW : (k + 1) * GW]] * (WIDE // GW), axis=0)
                table[index, k * WIDE : (k + 1) * WIDE, :] = jnp.where(
                    block_mask, tiled, 0.0
                ).astype(jnp.bfloat16)
            head = before[:, cols].astype(jnp.float32)
            tail = after[:, cols].astype(jnp.float32)
            pieces = []
            for w in range(windows):
                pieces += [
                    head[w * HALO : (w + 1) * HALO],
                    signal_ref[w, :, cols].astype(jnp.float32),
                    tail[w * HALO : (w + 1) * HALO],
                ]
            x = jnp.concatenate(pieces, axis=0)
            wide[:, cols] = x.astype(jnp.bfloat16)
            stack = jnp.concatenate(
                [shifted(x, 2 - k).astype(jnp.bfloat16) for k in range(KERNEL)], axis=1
            )
            value = jnp.dot(stack, table[index], preferred_element_type=jnp.float32)
            pre[:, cols] = local_part(value, windows, length)
            active = value / (1.0 + jnp.exp(-value))
            act[:, cols] = jnp.where(inside, active, 0.0).astype(jnp.bfloat16)
            return carry

        in_pairs(parts, encode)

    encode_from(me)
    for j in range(1, size):
        weight_copy(source[j], mine, across, 0, j, across).wait_recv()
        begin(weight_copy(source[j], across, across, 2, j, partner))
    for j in range(1, size):
        weight_copy(source[j], mine, partner, 1, j, partner).wait_recv()
        weight_copy(source[j], across, corner, 2, j, partner).wait_recv()
        encode_from(source[j])

    def decode(index, carry):
        cols = pl.ds(pl.multiple_of(index * WIDE, WIDE), WIDE)
        mixed = jnp.dot(act[...], onehot[:, cols], preferred_element_type=jnp.float32)
        decoded = jnp.zeros((rows, WIDE), jnp.float32)
        own_mixed = []
        for k in range(KERNEL):
            moved = shifted(mixed, k - 2)
            own_mixed.append(local_part(moved, windows, length).astype(jnp.bfloat16))
            decoded += lax.dot_general(
                moved.astype(jnp.bfloat16),
                table[index, k * WIDE : (k + 1) * WIDE, :],
                NT,
                preferred_element_type=jnp.float32,
            )
        error = jnp.where(inside, decoded - wide[:, cols].astype(jnp.float32), 0.0)
        own_decoded = local_part(decoded, windows, length).astype(jnp.bfloat16)
        for w in range(windows):
            rec_ref[w, :, cols] = own_decoded[w * length : (w + 1) * length]
        own_error = local_part(error, windows, length)
        square[...] += (own_error * own_error).reshape(-1, 8, WIDE).sum(axis=0)
        stack = jnp.concatenate(
            [shifted(error, 2 - k).astype(jnp.bfloat16) for k in range(KERNEL)], axis=1
        )
        value = jnp.dot(stack, table[index], preferred_element_type=jnp.float32)
        back[:, cols] = local_part(value, windows, length).astype(jnp.bfloat16)
        product = lax.dot_general(
            own_error.astype(jnp.bfloat16),
            jnp.concatenate(own_mixed, axis=1),
            TN,
            preferred_element_type=jnp.float32,
        )
        for k in range(KERNEL):
            partial[index, k * GW : (k + 1) * GW, :] = diagonal(
                product[:, k * WIDE : (k + 1) * WIDE]
            )
        return carry

    in_pairs(blocks, decode)

    def finish_for(owner):
        def finish(p, carry):
            index = owner * parts + p
            start = pl.multiple_of(index * WIDE, WIDE)
            cols = pl.ds(start, WIDE)
            restored = lax.dot_general(
                back[...], onehot[pl.ds(start, WIDE), :], NT, preferred_element_type=jnp.float32
            )
            value = pre[:, cols]
            sigma = 1.0 / (1.0 + jnp.exp(-value))
            own = (restored * (sigma * (1.0 + value * (1.0 - sigma)))).astype(jnp.bfloat16)
            for w in range(windows):
                back_ref[w, :, cols] = own[w * length : (w + 1) * length]
            spread = spread_part(own.astype(jnp.float32), windows, length)
            stack = jnp.concatenate(
                [shifted(spread, k - 2).astype(jnp.bfloat16) for k in range(KERNEL)], axis=1
            )
            product = lax.dot_general(wide[:, cols], stack, TN, preferred_element_type=jnp.float32)
            total = partial[index] + jnp.concatenate(
                [diagonal(product[:, k * WIDE : (k + 1) * WIDE]) for k in range(KERNEL)], axis=0
            )
            grad[owner, p] = total.reshape(members, quarter_rows, WIDE).astype(grad.dtype)
            return carry

        in_pairs(parts, finish)

    core, x = {}, {}

    def send_core_chunk(j):
        for slot, quarter in ((1, corner), (0, partner)):
            core[slot, j] = begin(
                remote(
                    grad.at[target[j], :, quarter], halves.at[slot, j], send_core.at[slot, j],
                    recv_core.at[slot, j], {"dp": partner},
                )
            )

    def send_x_chunk(j):
        core[1, j].wait_recv()
        passed[j] = (
            grad[target[j], :, across].astype(jnp.float32) + halves[1, j].astype(jnp.float32)
        ).astype(passed.dtype)
        x[j] = begin(
            remote(passed.at[j], crossed.at[j], send_x.at[j], recv_x.at[j], {"dp": across})
        )

    def send_tm_chunk(j):
        core[0, j].wait_recv()
        x[j].wait_recv()
        value = (
            grad[target[j], :, mine].astype(jnp.float32)
            + halves[0, j].astype(jnp.float32)
            + crossed[j].astype(jnp.float32)
        )
        if j == 0:
            own_total[...] = value
        else:
            kept[j] = value.astype(kept.dtype)
            begin(
                remote(
                    kept.at[j], incoming.at[j], send_tm.at[j], recv_tm.at[j], {"tm": target[j]}
                )
            )

    order = list(range(1, size)) + [0]
    for n in range(size + 2):
        if n < size:
            finish_for(target[order[n]])
            send_core_chunk(order[n])
        if 1 <= n <= size:
            send_x_chunk(order[n - 1])
        if n >= 2:
            send_tm_chunk(order[n - 2])

    total = own_total[...]
    for j in range(1, size):
        remote(
            kept.at[j], incoming.at[j], send_tm.at[j], recv_tm.at[j], {"tm": source[j]}
        ).wait_recv()
        total = total + incoming[j].astype(jnp.float32)
    rounded = total.astype(owned_ref.dtype)
    owned_ref[:, mine] = rounded

    def share(bit, quarter, number):
        return begin(
            remote(
                owned_ref.at[:, quarter], owned_ref.at[:, quarter], send_gather.at[number],
                recv_gather.at[number], {"dp": flip(mine, bit)},
            )
        )

    def take(bit, quarter, number):
        remote(
            owned_ref.at[:, flip(quarter, bit)], owned_ref.at[:, flip(quarter, bit)],
            send_gather.at[number], recv_gather.at[number], {"dp": flip(mine, bit)},
        ).wait_recv()

    back = rounded.astype(jnp.float32)
    powers = (back * back).reshape(-1, 8, back.shape[-1]).sum(axis=0)
    total_ref[...] = jnp.zeros_like(total_ref)
    width = powers.shape[-1]
    if width % 128 == 0:
        folded = powers[:, :128]
        for n in range(1, width // 128):
            folded = folded + powers[:, n * 128 : (n + 1) * 128]
        total_ref[8:16, :] = folded
    else:
        total_ref[8:16, :width] = powers
    total_ref[0:8, :] = square[:, :128] + square[:, 128:]
    tile_in[me] = total_ref[...]
    for j in range(1, size):
        begin(
            remote(
                total_ref, tile_in.at[me], send_tile.at[j], recv_tile.at[j], {"tm": target[j]}
            )
        )
    share(far, mine, 0)
    share(near, mine, 1)
    for j in range(1, size):
        remote(
            total_ref, tile_in.at[source[j]], send_tile.at[j], recv_tile.at[j], {"tm": source[j]}
        ).wait_recv()
    tiles[0] = tile_in[...].sum(axis=0)
    begin(remote(tiles.at[0], tiles.at[1], send_sum.at[0], recv_sum.at[0], {"dp": across}))
    take(far, mine, 0)
    share(near, across, 2)
    remote(tiles.at[0], tiles.at[1], send_sum.at[0], recv_sum.at[0], {"dp": across}).wait_recv()
    tiles[2] = tiles[0] + tiles[1]
    begin(remote(tiles.at[2], tiles.at[3], send_sum.at[1], recv_sum.at[1], {"dp": partner}))
    take(near, mine, 1)
    take(near, across, 2)
    remote(tiles.at[2], tiles.at[3], send_sum.at[1], recv_sum.at[1], {"dp": partner}).wait_recv()
    for copy in outgoing:
        copy.wait_send()
    sums = tiles[2] + tiles[3]
    count = windows * members * length * size * channels
    mean_ref[...] = jnp.sum(sums[:8], axis=(0, 1), keepdims=True) / count
    square_total = jnp.sum(sums[8:], axis=(0, 1), keepdims=True)
    for p in range(parts):
        lanes = slice(p * WIDE, (p + 1) * WIDE)
        for d in range(members):
            taken = slice(d * quarter_rows, (d + 1) * quarter_rows)
            direction_ref[taken, lanes] = adam_direction(
                owned_ref[p, d].astype(jnp.float32), square_total, KW * CH,
                weight_ref[taken, lanes], first_ref[taken, lanes], second_ref[taken, lanes],
            )


def fused_step(signal, weight, first_moment, second_moment, shuffle):
    size, members = lax.axis_size("tm"), lax.axis_size("dp")
    assert members == 4
    windows, length, channels = signal.shape
    depth, cols = weight.shape
    parts, blocks, quarter = cols // WIDE, channels // WIDE, depth // members
    own, rows = windows * length, windows * (length + 2 * HALO)
    vmem = pl.BlockSpec(memory_space=pltpu.VMEM)
    dma = pltpu.SemaphoreType.DMA
    kind = jnp.bfloat16
    piece = (parts, quarter, WIDE)
    everything = (size, parts, members, quarter, WIDE)
    edge = pltpu.VMEM((windows * HALO, channels), kind)
    return pl.pallas_call(
        functools.partial(fused_kernel, size, members, windows, length),
        out_shape=(
            jax.ShapeDtypeStruct(signal.shape, kind),
            jax.ShapeDtypeStruct((1, 1), jnp.float32),
            jax.ShapeDtypeStruct(weight.shape, jnp.float32),
            jax.ShapeDtypeStruct(signal.shape, kind),
        ),
        in_specs=[vmem] * 5,
        out_specs=(vmem,) * 4,
        scratch_shapes=[
            pltpu.VMEM((channels, channels), kind),
            pltpu.VMEM((blocks, KERNEL * WIDE, WIDE), kind),
            pltpu.VMEM((own, channels), jnp.float32),
            pltpu.VMEM((rows, channels), kind),
            pltpu.VMEM((own, channels), kind),
            pltpu.VMEM((blocks, depth, WIDE), jnp.float32),
            pltpu.VMEM((rows, channels), kind),
            pltpu.VMEM(everything, kind),
            edge, edge, edge, edge,
            pltpu.VMEM(everything, kind),
            pltpu.VMEM((8, WIDE), jnp.float32),
            pltpu.VMEM((2, size) + piece, kind),
            pltpu.VMEM((size,) + piece, kind),
            pltpu.VMEM((size,) + piece, kind),
            pltpu.VMEM((size,) + piece, kind),
            pltpu.VMEM((size,) + piece, kind),
            pltpu.VMEM(piece, jnp.float32),
            pltpu.VMEM((4, 16, 128), jnp.float32),
            pltpu.VMEM((size, 16, 128), jnp.float32),
            pltpu.VMEM((parts, members, quarter, WIDE), kind),
            pltpu.VMEM((16, 128), jnp.float32),
            dma((2,)), dma((2,)), dma((size,)), dma((size,)), dma((3, size)), dma((3, size)),
            dma((2, size)), dma((2, size)), dma((size,)), dma((size,)), dma((size,)),
            dma((size,)), dma((size,)), dma((size,)), dma((3,)), dma((3,)), dma((2,)), dma((2,)),
        ],
        compiler_params=pltpu.CompilerParams(
            collective_id=2, has_side_effects=True, vmem_limit_bytes=56 * 1024 * 1024
        ),
    )(signal, weight, first_moment, second_moment, shuffle.reshape(1, channels))


def adam_direction(grad_part, square_total, entries, weight_part, first_part, second_part):
    rms_value = jnp.sqrt(square_total / entries + rms_eps)
    factor = jnp.minimum(1.0, 1.0 / rms_value)
    clipped = grad_part * factor
    first_new = beta_one * first_part + (1.0 - beta_one) * clipped
    second_new = beta_two * second_part + (1.0 - beta_two) * clipped * clipped
    first_hat = first_new / (1.0 - beta_one**step_count)
    second_hat = second_new / (1.0 - beta_two**step_count)
    return first_hat / (jnp.sqrt(second_hat) + adam_eps) + decay_rate * weight_part


def on_device(signal, weight, first_moment, second_moment, shuffle):
    windows, length, channels = signal.shape
    size, members = lax.axis_size("tm"), lax.axis_size("dp")
    depth, cols = weight.shape
    width = WIDE if cols % WIDE == 0 else cols
    parts, blocks = cols // width, channels // WIDE
    rows = depth // members
    if cols % WIDE == 0:
        decoded, mean_error, direction, back_pre = fused_step(
            signal, weight, first_moment, second_moment, shuffle
        )
        return (decoded, mean_error.reshape(1), direction, back_pre)
    shard = weight.astype(jnp.bfloat16).reshape(members, rows, parts, width).transpose(2, 0, 1, 3)
    first = signal[:, :HALO].reshape(windows * HALO, channels)
    last = signal[:, length - HALO :].reshape(windows * HALO, channels)
    full, before, after = gather_step(shard, first, last)
    full = (
        full.reshape(blocks, WIDE // width, depth, width)
        .transpose(0, 2, 1, 3)
        .reshape(blocks, depth, WIDE)
    )
    before = before.reshape(windows, HALO, channels)
    after = after.reshape(windows, HALO, channels)
    decoded, back_pre, gradient, squares = local_step(signal, full, shuffle, before, after)
    gradient = (
        gradient.reshape(blocks, depth, WIDE // width, width)
        .transpose(0, 2, 1, 3)
        .reshape(size, parts, members, rows, width)
    )
    owned, totals = reduce_step(gradient, squares)
    element_count = windows * members * length * size * channels
    mean_error = (jnp.sum(totals[:8]) / element_count).reshape(1)
    owned = owned.transpose(1, 2, 0, 3).reshape(depth, cols).astype(jnp.float32)
    square_total = jnp.sum(totals[8:])
    direction = adam_direction(owned, square_total, KW * CH, weight, first_moment, second_moment)
    return (decoded, mean_error, direction, back_pre)


def solution(mesh):
    return jax.shard_map(
        on_device,
        mesh=mesh,
        in_specs=(
            P(("parts", "dp"), "tm", None),
            P("parts", "tm"),
            P("parts", "tm"),
            P("parts", "tm"),
            P(),
        ),
        out_specs=(
            P(("parts", "dp"), "tm", None),
            P("parts"),
            P("parts", "tm"),
            P(("parts", "dp"), "tm", None),
        ),
        check_vma=False,
    )
```
